128 devices in a mesh: blocks: 16 (over z, y), depth: 8 (over x, core).
Axes of the slice: x: 4, y: 4, z: 4, core: 2. Of those that a mesh axis runs over, the one named last changes fastest.
Arguments:
- estimate0: float32 [512, 512, 128], P('depth', 'blocks'), may hold values from 0.5 to 1.5
- tiles: float32 [128, 512, 8, 128], P('blocks', 'depth'), may hold values from 0.2 to 2
- psf_z: float32 [6, 61], replicated
- psf_x: float32 [6, 31], replicated
- psf_y: float32 [6, 31], replicated
- tile_pair: int32 [128], P('blocks'), may hold values from 0 to 383, as said below
- tile_shift: int32 [128], P('blocks'), may hold values from -8 to 8
Outputs:
- estimate: float32 [512, 512, 128], P('depth', 'blocks')
The draws below stay inside these ranges and needn't reach their ends.
Inputs may be any that keep to these rules, and one draw needn't show every extreme that they name: `tile_pair`: each entry is view * 64 + block for one of 6 views and one of 64 joined blocks; no pair appears twice and every block appears. Block b belongs to blocks index b // 4. Of the 8 tiles held by one blocks index, at most 1 belong to the blocks of any one blocks index, and some holder reaches 1; the tiles of one blocks index's blocks number at most 16 in all, and some blocks index has 16.
All inputs are finite; a program needn't handle non-finite values.
Results may differ from the reference program's by a relative error of at most 0.0003.
Values sent between devices are 32-bit elements; how exact they have to be, the bound alone decides.
No kernel may reach another device: no remote copies, remote signals or barrier semaphores. Data moves between devices by JAX's collectives and lax.ppermute only.
A program may use at most 128 MiB of HBM per device.

```python
import jax
import jax.numpy as jnp
from jax import lax

V = 6
KZ = 61
KX = 31
KY = 31
HZ = 30
HX = 15
HY = 15
NY = 128
BX = 8
BLK_DEV = 4
OFF = 8
ITERS = 2
TILES_DEV = 8
NBLK = 64
NT = 128
CAP = 1
NZ = 512
NX = 512


def kernel_profile(key, taps, rate):
    half = (taps - 1) // 2
    rough = jnp.exp(jax.random.uniform(key, (V, taps), jnp.float32, jnp.log(0.5), jnp.log(2.0)))
    reach = jnp.abs(jnp.arange(taps, dtype=jnp.float32) - half)
    return rough * jnp.exp(-reach * rate / max(half, 1))[None, :]


def draw_psf_z(key, part):
    key = jax.random.fold_in(key, 1)
    rate = 2.5
    return kernel_profile(key, KZ, rate)


def draw_psf_x(key, part):
    key = jax.random.fold_in(key, 2)
    rate = 2.5
    return kernel_profile(key, KX, rate)


def draw_psf_y(key, part):
    key = jax.random.fold_in(key, 3)
    rate = 2.5
    return kernel_profile(key, KY, rate)


def draw_tile_pair(key, part):
    key = jax.random.fold_in(key, 7)
    owner_key, view_key, deal_key, place_key = jax.random.split(key, 4)
    owners = NBLK // BLK_DEV
    pattern = jnp.array([4, 2, 1, 1], jnp.int32)
    ranking = jax.random.permutation(owner_key, owners)
    cover_owner = pattern[ranking % 4]
    cover_block = jnp.repeat(cover_owner, BLK_DEV)
    view_order = jax.vmap(lambda sub: jax.random.permutation(sub, V))(jax.random.split(view_key, NBLK))
    keeping = (jnp.arange(V)[None, :] < cover_block[:, None]).reshape(-1)
    codes = (view_order * NBLK + jnp.arange(NBLK)[:, None]).reshape(-1).astype(jnp.int32)
    ranked = jnp.cumsum(keeping.astype(jnp.int32)) - 1
    target = jnp.where(keeping, ranked, NT)
    ordered = jnp.zeros(NT, jnp.int32).at[target].set(codes, mode='drop')
    offset = jax.random.randint(deal_key, (), 0, owners)
    position = jnp.arange(NT)
    group = position // CAP
    holder = (group + offset) % owners
    within = CAP * (group // owners) + position % CAP
    shuffle = jax.vmap(lambda sub: jax.random.permutation(sub, TILES_DEV))(jax.random.split(place_key, owners))
    placed = holder * TILES_DEV + shuffle[holder, within]
    return jnp.zeros(NT, jnp.int32).at[placed].set(ordered)


def place_ends(values, stream_key, smallest, largest):
    extent = values.shape
    index_at = [jax.random.randint(jax.random.fold_in(stream_key, axis), (), 0, extent[axis]) for axis in range(len(extent))]
    values = values.at[tuple(index_at)].set(smallest)
    longest = extent.index(max(extent))
    index_at[longest] = (index_at[longest] + 1) % extent[longest]
    return values.at[tuple(index_at)].set(largest)


def shard_levels(rng, dims, pieces, smallest, high):
    def one(dim, blocks):
        steps = jax.random.uniform(jax.random.fold_in(jax.random.fold_in(rng, 6), dim), (blocks,), jnp.float32, smallest / len(pieces), high / len(pieces))
        return jnp.repeat(jnp.exp(steps), dims[dim] // blocks).reshape((-1,) + (1,) * (len(dims) - dim - 1))

    loudness = one(*pieces[0])
    for cut in pieces[1:]:
        loudness = loudness * one(*cut)
    return loudness


def setup_inputs(seed: int = 0) -> dict:
    key_of = jax.random.split(jax.random.key(seed), 8)
    return {
        "estimate0": jnp.clip(0.5 + 1.0 * jax.random.uniform(key_of[0], (NZ, NX, NY), jnp.float32) ** shard_levels(key_of[0], (NZ, NX, NY), ((0, 8), (1, 16)), -0.2, 0.2), 0.5, 1.5),
        "tiles": jnp.clip(0.2 + 1.8 * jax.random.uniform(key_of[1], (NT, NZ, BX, NY), jnp.float32) ** shard_levels(key_of[1], (NT, NZ, BX, NY), ((0, 16), (1, 8)), -0.2, 0.2), 0.2, 2.0),
        "psf_z": draw_psf_z(jax.random.fold_in(key_of[7], 71), 0),
        "psf_x": draw_psf_x(jax.random.fold_in(key_of[7], 71), 0),
        "psf_y": draw_psf_y(jax.random.fold_in(key_of[7], 71), 0),
        "tile_pair": draw_tile_pair(jax.random.fold_in(key_of[7], 71), 0),
        "tile_shift": place_ends(jax.random.randint(key_of[6], (NT,), -OFF, OFF + 1), jax.random.fold_in(key_of[6], 1), -OFF, OFF).astype(jnp.int32),
    }


def forward_slab(slab, kern_z, kern_x, kern_y):
    zsum = kern_z[0] * slab[0:NZ]
    for position in range(1, KZ):
        zsum = zsum + kern_z[position] * slab[position:position + NZ]
    xsum = kern_x[0] * zsum[:, 0:BX]
    for position in range(1, KX):
        xsum = xsum + kern_x[position] * zsum[:, position:position + BX]
    ysum = kern_y[0] * xsum[:, :, 0:NY]
    for position in range(1, KY):
        ysum = ysum + kern_y[position] * xsum[:, :, position:position + NY]
    return ysum


def backward_slab(ratio, kern_z, kern_x, kern_y):
    ypad = jnp.pad(ratio, ((0, 0), (0, 0), (KY - 1, KY - 1)))
    ysum = kern_y[0] * ypad[:, :, KY - 1:KY - 1 + NY + KY - 1]
    for position in range(1, KY):
        ysum = ysum + kern_y[position] * ypad[:, :, KY - 1 - position:KY - 1 - position + NY + KY - 1]
    xpad = jnp.pad(ysum, ((0, 0), (KX - 1, KX - 1), (0, 0)))
    xsum = kern_x[0] * xpad[:, KX - 1:KX - 1 + BX + KX - 1]
    for position in range(1, KX):
        xsum = xsum + kern_x[position] * xpad[:, KX - 1 - position:KX - 1 - position + BX + KX - 1]
    zpad = jnp.pad(xsum, ((KZ - 1, KZ - 1), (0, 0), (0, 0)))
    zsum = kern_z[0] * zpad[KZ - 1:KZ - 1 + NZ + KZ - 1]
    for position in range(1, KZ):
        zsum = zsum + kern_z[position] * zpad[KZ - 1 - position:KZ - 1 - position + NZ + KZ - 1]
    return zsum


def reference(estimate0, tiles, psf_z, psf_x, psf_y, tile_pair, tile_shift):
    kernel_z = psf_z / jnp.sum(psf_z, axis=1, keepdims=True)
    kernel_x = psf_x / jnp.sum(psf_x, axis=1, keepdims=True)
    kernel_y = psf_y / jnp.sum(psf_y, axis=1, keepdims=True)
    view_ids = tile_pair // NBLK
    block_ids = tile_pair % NBLK
    columns = jnp.arange(NY).astype(jnp.int32)
    anchor = jnp.zeros((), jnp.int32)

    def register(record, shift_value):
        padded = jnp.pad(record, ((0, 0), (0, 0), (OFF, OFF)))
        start = (OFF - shift_value).astype(jnp.int32)
        moved = lax.dynamic_slice_in_dim(padded, start, NY, 2)
        inside = ((columns >= shift_value) & (columns < NY + shift_value)).astype(jnp.float32)
        return moved * inside, inside

    def project(field_pad, use_data):
        def visit(total, item):
            record, view_id, block_id, shift_value = item
            kern_z = kernel_z[view_id]
            kern_x = kernel_x[view_id]
            kern_y = kernel_y[view_id]
            data, inside = register(record, shift_value)
            start = (block_id * BX).astype(jnp.int32)
            if use_data:
                slab = lax.dynamic_slice(field_pad, (anchor, start, anchor), (NZ + 2 * HZ, BX + 2 * HX, NY + 2 * HY))
                ratio = data / forward_slab(slab, kern_z, kern_x, kern_y)
            else:
                ratio = jnp.broadcast_to(inside, (NZ, BX, NY))
            part = backward_slab(ratio, kern_z, kern_x, kern_y)
            current = lax.dynamic_slice(total, (anchor, start, anchor), part.shape)
            return lax.dynamic_update_slice(total, current + part, (anchor, start, anchor)), None

        empty = jnp.zeros((NZ + 2 * HZ, NX + 2 * HX, NY + 2 * HY), jnp.float32)
        total, _ = lax.scan(visit, empty, (tiles, view_ids, block_ids, tile_shift))
        return total[HZ:HZ + NZ, HX:HX + NX, HY:HY + NY]

    weight = jnp.maximum(project(None, False), 1.0)
    estimate = estimate0
    for sweep in range(ITERS):
        padded = jnp.pad(estimate, ((HZ, HZ), (HX, HX), (HY, HY)))
        estimate = estimate * project(padded, True) / weight
    return estimate
```

```python
import functools

import jax
import jax.numpy as jnp
from jax import lax
from jax.experimental import pallas as pl
from jax.experimental.pallas import tpu as pltpu
from jax.sharding import PartitionSpec as P

BLK_DEV = 4
BX = 8
OFF = 8
ITERS = 2
V = 6
NY = 128
DZ = 64
DX = 32
RZ = 30
PZ = 32
RX = 16
EZ = DZ + 2 * PZ
EX = DX + 2 * RX
ROWS = V * DX
MIB = 1 << 20

exact_mode = lax.Precision.HIGHEST


def split(value):
    high = value.astype(jnp.bfloat16)
    low = (value - high.astype(jnp.float32)).astype(jnp.bfloat16)
    return high, low


def mul(a, b):
    return jnp.dot(a, b, preferred_element_type=jnp.float32)


def pair_columns(value, rows):
    return value[:, : value.shape[1] // 2], value[:, value.shape[1] // 2 :]


def blur_x(xf, planes, store):
    both = jnp.concatenate(planes, axis=1)
    high, low = split(both)
    out = mul(xf, jnp.concatenate([high, low, high], axis=0))
    store(out[:, :NY], out[:, NY:])


def forward_x(s_ref, xf_ref, est, left, right, topc, tops, botc, bots):
    zeros = jnp.zeros((2, ROWS, NY), jnp.float32)
    s_ref[0:2] = zeros
    s_ref[EZ - 2 : EZ] = zeros

    def put(base):
        def store(first, second):
            s_ref[base] = first
            s_ref[base + 1] = second

        return store

    def rim(centre, sides, start):
        @pl.loop(0, RZ // 2)
        def _(k):
            planes = []
            for z in (2 * k, 2 * k + 1):
                planes.append(
                    jnp.concatenate([sides[z, :RX], centre[z], sides[z, RX:]], axis=0)
                )
            blur_x(xf_ref[...], planes, put(start + 2 * k))

    @pl.loop(0, DZ // 2)
    def _(k):
        planes = []
        for z in (2 * k, 2 * k + 1):
            planes.append(jnp.concatenate([left[z], est[z], right[z]], axis=0))
        blur_x(xf_ref[...], planes, put(PZ + 2 * k))

    rim(topc, tops, PZ - RZ)
    rim(botc, bots, PZ + DZ)


def shifted_y(yt_ref, view, shift):
    table = yt_ref[view, pl.ds(OFF + shift, NY), :]
    row = lax.broadcasted_iota(jnp.int32, (NY, NY), 0) + shift
    return split(jnp.where((row >= 0) & (row < NY), table, 0.0))


def forward_tile(s_ref, zf_ref, table, view, row):
    field = jnp.swapaxes(s_ref[:, pl.ds(row, BX), :], 0, 1)
    parts = []
    for p in range(BX // 2):
        high, low = split(jnp.concatenate([field[2 * p], field[2 * p + 1]], axis=1))
        out = mul(zf_ref[view], jnp.concatenate([high, low], axis=0))
        out = out[:DZ] + out[DZ:]
        parts += [out[:, :NY], out[:, NY:]]
    high, low = split(jnp.concatenate(parts, axis=0))
    whigh, wlow = table
    rhs = jnp.concatenate(
        [jnp.concatenate([whigh, whigh], axis=1), jnp.concatenate([wlow, wlow], axis=1)], axis=0
    )
    out = lax.dot_general(
        jnp.concatenate([high, low], axis=1),
        rhs,
        (((1,), (1,)), ((), ())),
        preferred_element_type=jnp.float32,
    )
    return out[:, :NY] + out[:, NY:]


def ratio_of(record, predicted, shift):
    data = jnp.swapaxes(record, 0, 1).reshape(BX * DZ, NY)
    lane = lax.broadcasted_iota(jnp.int32, (BX * DZ, NY), 1) + shift
    inside = (lane >= 0) & (lane < NY)
    return jnp.where(inside, data / jnp.where(inside, predicted, 1.0), 0.0)


def backward_tile(s_ref, zb_ref, table, view, row, ratio):
    whigh, wlow = table
    high, low = split(ratio)
    half = jnp.concatenate([whigh, wlow], axis=1)
    out = mul(jnp.concatenate([high, low], axis=1), jnp.concatenate([half, half], axis=0))
    out = out[:, :NY] + out[:, NY:]
    parts = []
    for p in range(BX // 2):
        first = out[2 * p * DZ : (2 * p + 1) * DZ]
        second = out[(2 * p + 1) * DZ : (2 * p + 2) * DZ]
        high, low = split(jnp.concatenate([first, second], axis=1))
        res = mul(zb_ref[view], jnp.concatenate([high, low, high], axis=0))
        parts += [res[:, :NY], res[:, NY:]]
    s_ref[:, pl.ds(row, BX), :] = jnp.swapaxes(jnp.stack(parts, axis=0), 0, 1)


def backward_x(s_ref, xb_ref, midc, midl, midr, topc, tops, botc, bots):
    def spread_pair(base):
        both = jnp.concatenate([s_ref[base], s_ref[base + 1]], axis=1)
        high, low = split(both)
        out = mul(xb_ref[...], jnp.concatenate([high, low], axis=0))
        out = out[:EX] + out[EX:]
        return out[:, :NY], out[:, NY:]

    def rim(centre, sides, start):
        @pl.loop(0, RZ // 2)
        def _(k):
            for i, plane in enumerate(spread_pair(start + 2 * k)):
                z = 2 * k + i
                sides[z] = jnp.concatenate([plane[:RX], plane[RX + DX :]], axis=0)
                centre[z] = plane[RX : RX + DX]

    rim(topc, tops, PZ - RZ)
    rim(botc, bots, PZ + DZ)

    @pl.loop(0, DZ // 2)
    def _(k):
        for i, plane in enumerate(spread_pair(PZ + 2 * k)):
            z = 2 * k + i
            midl[z] = plane[:RX]
            midc[z] = plane[RX : RX + DX]
            midr[z] = plane[RX + DX :]


def sweep_body(slots, meta, est, left, right, topc, tops, botc, bots, data, xf, xb, zf, zb, yt,
               omidc, omidl, omidr, otopc, otops, obotc, obots, s_ref):
    forward_x(s_ref, xf, est, left, right, topc, tops, botc, bots)

    @pl.loop(0, V * BLK_DEV)
    def _(pair):
        @pl.when(meta[4 * slots + pair] == 0)
        def _():
            s_ref[:, pl.ds(pl.multiple_of(pair * BX, BX), BX), :] = jnp.zeros(
                (EZ, BX, NY), jnp.float32
            )

    @pl.loop(0, slots)
    def _(slot):
        view = meta[slots + slot]
        row = pl.multiple_of(view * DX + meta[2 * slots + slot] * BX, BX)
        shift = meta[3 * slots + slot]

        @pl.when(meta[slot] > 0)
        def _():
            table = shifted_y(yt, view, shift)
            predicted = forward_tile(s_ref, zf, table, view, row)
            ratio = ratio_of(data[slot], predicted, shift)
            backward_tile(s_ref, zb, table, view, row, ratio)

    backward_x(s_ref, xb, omidc, omidl, omidr, otopc, otops, obotc, obots)


def f32(*shape):
    return jax.ShapeDtypeStruct(shape, jnp.float32)


VM = pl.BlockSpec(memory_space=pltpu.VMEM)
SM = pl.BlockSpec(memory_space=pltpu.SMEM)
PIECES = (
    f32(DZ, DX, NY),
    f32(DZ, RX, NY),
    f32(DZ, RX, NY),
    f32(RZ, DX, NY),
    f32(RZ, 2 * RX, NY),
    f32(RZ, DX, NY),
    f32(RZ, 2 * RX, NY),
)


def sweep(meta, pieces, data, tables):
    slots = data.shape[0]
    return pl.pallas_call(
        functools.partial(sweep_body, slots),
        out_shape=PIECES,
        in_specs=[SM] + [VM] * 13,
        out_specs=[VM] * 7,
        scratch_shapes=[pltpu.VMEM((EZ, ROWS, NY), jnp.float32)],
        compiler_params=pltpu.CompilerParams(vmem_limit_bytes=56 * MIB),
        name="sweep",
    )(meta, *pieces, data, *tables)


def place_body(where, tiles, out, sem):
    count = where.shape[0]
    for slot in range(count):

        @pl.when(where[slot] >= 0)
        def _():
            pltpu.make_async_copy(tiles.at[where[slot]], out.at[slot], sem.at[slot]).start()

    for slot in range(count):

        @pl.when(where[slot] >= 0)
        def _():
            pltpu.make_async_copy(tiles.at[where[slot]], out.at[slot], sem.at[slot]).wait()


def place(where, tiles):
    count = where.shape[0]
    return pl.pallas_call(
        place_body,
        out_shape=f32(count, *tiles.shape[1:]),
        in_specs=[SM, VM],
        out_specs=pl.BlockSpec(memory_space=pl.ANY),
        scratch_shapes=[pltpu.SemaphoreType.DMA((count,))],
        compiler_params=pltpu.CompilerParams(vmem_limit_bytes=32 * MIB),
        name="place",
    )(where, tiles)


def rims_body(midl, midr, above, below, outl, outr):
    for mid, out, at in ((midl, outl, 0), (midr, outr, RX)):
        cols = pl.ds(at, RX)
        out[:RZ] = mid[:RZ] + above[:, cols]
        out[RZ : DZ - RZ] = mid[RZ : DZ - RZ]
        out[DZ - RZ :] = mid[DZ - RZ :] + below[:, cols]


def fold_rims(midl, midr, above, below):
    return pl.pallas_call(
        rims_body,
        out_shape=(f32(DZ, RX, NY), f32(DZ, RX, NY)),
        in_specs=[VM] * 4,
        out_specs=[VM] * 2,
        compiler_params=pltpu.CompilerParams(vmem_limit_bytes=32 * MIB),
        name="fold_rims",
    )(midl, midr, above, below)


def update_body(wz, est, midc, above, below, froml, fromr, gain, *outs):
    def step(z, extra):
        total = midc[z]
        if extra is not None:
            total = total + extra
        total = total + jnp.concatenate([froml[z], fromr[z]], axis=0)
        weight = wz[0, z] * gain[0]
        for view in range(1, V):
            weight = weight + wz[view, z] * gain[view]
        return est[z] * total / jnp.maximum(weight, 1.0)

    def write(z, new):
        outs[0][z] = new
        if len(outs) > 1:
            outs[1][z] = new[:RX]
            outs[2][z] = new[RX:]

    @pl.loop(0, RZ)
    def _(z):
        new = step(z, above[z])
        write(z, new)
        if len(outs) > 1:
            outs[3][z] = new

    for z in range(RZ, DZ - RZ):
        write(z, step(z, None))

    @pl.loop(0, RZ)
    def _(k):
        new = step(k + DZ - RZ, below[k])
        write(k + DZ - RZ, new)
        if len(outs) > 1:
            outs[4][k] = new


def update(wz, est, midc, above, below, froml, fromr, gain, last):
    shapes = [f32(DZ, DX, NY)]
    if not last:
        shapes += [f32(DZ, RX, NY)] * 2 + [f32(RZ, DX, NY)] * 2
    return pl.pallas_call(
        update_body,
        out_shape=tuple(shapes),
        in_specs=[SM] + [VM] * 7,
        out_specs=[VM] * len(shapes),
        compiler_params=pltpu.CompilerParams(vmem_limit_bytes=32 * MIB),
        name="update",
    )(wz, est, midc, above, below, froml, fromr, gain)


def band(row, rows, first):
    table = jnp.broadcast_to(row, (rows, row.shape[1]))
    return pltpu.roll(table, first % row.shape[1], 1, stride=1, stride_axis=0)


def tables_body(kz, kx, ky, xf, xb, zf, zb, yt):
    for view in range(V):
        full = band(kz[view : view + 1], DZ, PZ - RZ)
        high, low = split(full)
        zf[view] = jnp.concatenate(
            [jnp.concatenate([high, high], axis=1), jnp.concatenate([low, low], axis=1)], axis=0
        )
        high, low = split(full.T)
        zb[view] = jnp.concatenate([high, high, low], axis=1)
        yt[view] = band(ky[view : view + 1], NY + 2 * OFF, -15 - OFF)[:, :NY]
    full = jnp.concatenate([band(kx[v : v + 1], DX, RX - 15) for v in range(V)], axis=0)
    high, low = split(full[:, :EX])
    xf[...] = jnp.concatenate([high, high, low], axis=1)
    high, low = split(full.T[:EX])
    both = jnp.concatenate([high, low], axis=0)
    xb[...] = jnp.concatenate([both, both], axis=1)


def make_tables(kernel_z, kernel_x, kernel_y):
    def bf16(*shape):
        return jax.ShapeDtypeStruct(shape, jnp.bfloat16)

    def padded(kernel, lanes):
        return jnp.pad(kernel, ((0, 8 - V), (0, lanes - kernel.shape[1])))

    return pl.pallas_call(
        tables_body,
        out_shape=(
            bf16(ROWS, 3 * EX),
            bf16(2 * EX, 2 * ROWS),
            bf16(V, 2 * DZ, 2 * EZ),
            bf16(V, EZ, 3 * DZ),
            f32(V, NY + 2 * OFF, NY),
        ),
        in_specs=[VM] * 3,
        out_specs=[VM] * 5,
        compiler_params=pltpu.CompilerParams(vmem_limit_bytes=32 * MIB),
        name="tables",
    )(padded(kernel_z, 128), padded(kernel_x, 128), padded(kernel_y, 256))


def send(value, axis, step):
    count = lax.axis_size(axis)
    if step > 0:
        pairs = [(i, i + 1) for i in range(count - 1)]
    else:
        pairs = [(i + 1, i) for i in range(count - 1)]
    return lax.ppermute(value, axis, pairs)


def halo(est, coll, colr, planet, planeb):
    right = send(coll, "blocks", -1)
    left = send(colr, "blocks", 1)
    botc = send(planet, "depth", -1)
    topc = send(planeb, "depth", 1)
    sides_t = jnp.concatenate([left[:RZ], right[:RZ]], axis=1)
    sides_b = jnp.concatenate([left[DZ - RZ :], right[DZ - RZ :]], axis=1)
    bots = send(sides_t, "depth", -1)
    tops = send(sides_b, "depth", 1)
    return est, left, right, topc, tops, botc, bots


def weight_parts(pairs, shifts, kernel_z, kernel_x, kernel_y, yt, all_blocks):
    planes = lax.axis_size("depth") * DZ
    view = pairs // all_blocks
    block = pairs % all_blocks
    taps = jnp.arange(kernel_z.shape[1])[None, :]
    z = lax.axis_index("depth") * DZ + jnp.arange(DZ)[:, None]
    reached = ((z - taps + RZ >= 0) & (z - taps + RZ < planes)).astype(jnp.float32)
    wz = jnp.einsum("va,za->vz", kernel_z, reached, precision=exact_mode)
    hot = (view[:, None] == jnp.arange(V)[None, :]).astype(jnp.float32)
    x = lax.axis_index("blocks") * DX + jnp.arange(DX)
    lead = x[None, :, None] + 15 - BX * block[:, None, None] - jnp.arange(kernel_x.shape[1])[None, None, :]
    covers = ((lead >= 0) & (lead < BX)).astype(jnp.float32)
    along_x = jnp.einsum("txb,vb->vtx", covers, kernel_x, precision=exact_mode) * hot.T[:, :, None]
    y = jnp.arange(NY)
    inside = (y[None, :] >= shifts[:, None]) & (y[None, :] < NY + shifts[:, None])
    along_y = jnp.einsum("ty,vyc->vtc", inside.astype(jnp.float32), yt[:, OFF : OFF + NY], precision=exact_mode)
    gain = jnp.einsum("vtx,vtc->vxc", along_x, along_y, precision=exact_mode)
    return wz, gain


def local(estimate0, tiles, psf_z, psf_x, psf_y, tile_pair, tile_shift):
    owners = lax.axis_size("blocks")
    all_blocks = BLK_DEV * owners
    me = lax.axis_index("blocks")
    kernel_z = psf_z / jnp.sum(psf_z, axis=1, keepdims=True)
    kernel_x = psf_x / jnp.sum(psf_x, axis=1, keepdims=True)
    kernel_y = psf_y / jnp.sum(psf_y, axis=1, keepdims=True)

    held = tile_pair % all_blocks // BLK_DEV
    number = jnp.arange(tiles.shape[0])
    goes = held[None, :] == jnp.arange(owners)[:, None]
    where = jnp.max(jnp.where(goes, number[None, :], -1), axis=1)
    got = lax.all_to_all(place(where, tiles), "blocks", split_axis=0, concat_axis=0, tiled=True)

    packed = tile_pair * 32 + (tile_shift + OFF)
    everyone = lax.all_gather(packed, "blocks", axis=0, tiled=True)
    pairs = everyone // 32
    shifts = everyone % 32 - OFF
    mine = (pairs % all_blocks // BLK_DEV == me).reshape(owners, -1)
    live = jnp.max(mine.astype(jnp.int32), axis=1)
    got_pair = jnp.sum(jnp.where(mine, pairs.reshape(owners, -1), 0), axis=1)
    got_shift = jnp.sum(jnp.where(mine, shifts.reshape(owners, -1), 0), axis=1)
    got_view = got_pair // all_blocks
    got_block = jnp.where(live > 0, got_pair % all_blocks - me * BLK_DEV, 0)
    cell = got_view * BLK_DEV + got_block
    present = jnp.max(
        jnp.where(cell[None, :] == jnp.arange(V * BLK_DEV)[:, None], live[None, :], 0), axis=1
    )
    meta = jnp.concatenate([live, got_view, got_block, got_shift, present]).astype(jnp.int32)

    tables = make_tables(kernel_z, kernel_x, kernel_y)
    wz, gain = weight_parts(pairs, shifts, kernel_z, kernel_x, kernel_y, tables[4], all_blocks)

    est = estimate0
    rims = (est[:, :RX], est[:, DX - RX :], est[:RZ], est[DZ - RZ :])
    for iteration in range(ITERS):
        pieces = halo(est, *rims)
        midc, midl, midr, topc, tops, botc, bots = sweep(meta, pieces, got, tables)
        below_s = send(tops, "depth", -1)
        above_s = send(bots, "depth", 1)
        below_c = send(topc, "depth", -1)
        above_c = send(botc, "depth", 1)
        rim_l, rim_r = fold_rims(midl, midr, above_s, below_s)
        fromr = send(rim_l, "blocks", -1)
        froml = send(rim_r, "blocks", 1)
        est, *rims = update(
            wz, est, midc, above_c, below_c, froml, fromr, gain, iteration == ITERS - 1
        )
    return est


def solution(mesh):
    in_specs = (
        P("depth", "blocks", None),
        P("blocks", "depth", None, None),
        P(),
        P(),
        P(),
        P("blocks"),
        P("blocks"),
    )
    out_specs = P("depth", "blocks", None)
    return jax.shard_map(local, mesh=mesh, in_specs=in_specs, out_specs=out_specs, check_vma=False)
```

```python
import functools

import jax
import jax.numpy as jnp
from jax import lax
from jax.experimental import pallas as pl
from jax.experimental.pallas import tpu as pltpu
from jax.sharding import PartitionSpec as P

BLK_DEV = 4
BX = 8
OFF = 8
ITERS = 2
V = 6
NY = 128
DZ = 64
DX = 32
RZ = 30
PZ = 32
RX = 16
EZ = DZ + 2 * PZ
EX = DX + 2 * RX
ROWS = V * DX
MIB = 1 << 20

exact_mode = lax.Precision.HIGHEST


def split(value):
    high = value.astype(jnp.bfloat16)
    low = (value - high.astype(jnp.float32)).astype(jnp.bfloat16)
    return high, low


def mul(a, b):
    return jnp.dot(a, b, preferred_element_type=jnp.float32)


def pair_columns(value, rows):
    return value[:, : value.shape[1] // 2], value[:, value.shape[1] // 2 :]


def blur_x(xf, planes, store):
    both = jnp.concatenate(planes, axis=1)
    high, low = split(both)
    out = mul(xf, jnp.concatenate([high, low, high], axis=0))
    store(out[:, :NY], out[:, NY:])


def forward_x(s_ref, xf_ref, est, left, right, topc, tops, botc, bots):
    zeros = jnp.zeros((2, ROWS, NY), jnp.float32)
    s_ref[0:2, :ROWS] = zeros
    s_ref[EZ - 2 : EZ, :ROWS] = zeros

    def put(base):
        def store(first, second):
            s_ref[base, :ROWS] = first
            s_ref[base + 1, :ROWS] = second

        return store

    def rim(centre, sides, start):
        @pl.loop(0, RZ // 6)
        def _(group):
            for u in range(3):
                at = 6 * group + 2 * u
                planes = []
                for z in (at, at + 1):
                    planes.append(
                        jnp.concatenate([sides[z, :RX], centre[z], sides[z, RX:]], axis=0)
                    )
                blur_x(xf_ref[...], planes, put(start + at))

    @pl.loop(0, DZ // 8)
    def _(group):
        for u in range(4):
            at = 8 * group + 2 * u
            planes = []
            for z in (at, at + 1):
                planes.append(jnp.concatenate([left[z], est[z], right[z]], axis=0))
            blur_x(xf_ref[...], planes, put(PZ + at))

    rim(topc, tops, PZ - RZ)
    rim(botc, bots, PZ + DZ)


def halves(value):
    middle = value.shape[1] // 2
    return value[:, :middle], value[:, middle:]


def forward_tile(s_ref, zf_ref, yf_ref, view, row):
    field = jnp.swapaxes(s_ref[:, pl.ds(row, BX), :], 0, 1)
    parts = []
    for p in range(BX // 2):
        high, low = split(jnp.concatenate([field[2 * p], field[2 * p + 1]], axis=1))
        out = mul(zf_ref[view], jnp.concatenate([high, low], axis=0))
        parts += halves(out[:DZ] + out[DZ:])
    high, low = split(jnp.concatenate(parts, axis=0))
    first, second = halves(mul(jnp.concatenate([high, low], axis=1), yf_ref[view]))
    return first + second


def backward_tile(zb_ref, yb_ref, view, ratio):
    high, low = split(ratio)
    first, second = halves(mul(jnp.concatenate([high, low], axis=1), yb_ref[view]))
    out = first + second
    parts = []
    for p in range(BX // 2):
        at = 2 * p * DZ
        high, low = split(jnp.concatenate([out[at : at + DZ], out[at + DZ : at + 2 * DZ]], axis=1))
        parts += halves(mul(zb_ref[view], jnp.concatenate([high, low, high], axis=0)))
    return jnp.swapaxes(jnp.stack(parts, axis=0), 0, 1)


def backward_x(s_ref, xb_ref, midc, midl, midr, topc, tops, botc, bots):
    def spread_pair(base):
        both = jnp.concatenate([s_ref[base, :ROWS], s_ref[base + 1, :ROWS]], axis=1)
        high, low = split(both)
        out = mul(xb_ref[...], jnp.concatenate([high, low], axis=0))
        return halves(out[:EX] + out[EX:])

    def rim(centre, sides, start):
        @pl.loop(0, RZ // 6)
        def _(group):
            for u in range(3):
                at = 6 * group + 2 * u
                for i, plane in enumerate(spread_pair(start + at)):
                    sides[at + i] = jnp.concatenate([plane[:RX], plane[RX + DX :]], axis=0)
                    centre[at + i] = plane[RX : RX + DX]

    rim(topc, tops, PZ - RZ)
    rim(botc, bots, PZ + DZ)

    @pl.loop(0, DZ // 8)
    def _(group):
        for u in range(4):
            at = 8 * group + 2 * u
            for i, plane in enumerate(spread_pair(PZ + at)):
                midl[at + i] = plane[:RX]
                midc[at + i] = plane[RX : RX + DX]
                midr[at + i] = plane[RX + DX :]


def compact(slots, meta, order):
    count = jnp.int32(0)
    for slot in range(slots):
        order[count] = slot
        count = count + meta[slot]
    order[count] = slots
    return count


def clear_absent(slots, meta, s_ref):
    @pl.loop(0, V * BLK_DEV)
    def _(cell):
        @pl.when(meta[3 * (slots + 1) + cell] == 0)
        def _():
            s_ref[:, pl.ds(pl.multiple_of(cell * BX, BX), BX), :] = jnp.zeros(
                (EZ, BX, NY), jnp.float32
            )


def visit_pairs(slots, meta, order, s_ref, data, zb, yb, predict):
    count = compact(slots, meta, order)

    @pl.loop(0, (count + 1) // 2)
    def _(k):
        slot = (order[2 * k], order[2 * k + 1])
        view = [meta[slots + 1 + i] for i in slot]
        cell = [meta[2 * (slots + 1) + i] for i in slot]
        row = [pl.multiple_of(i * BX, BX) for i in cell]
        blurred = [predict(view[i], cell[i], row[i]) for i in (0, 1)]
        ratio = [data[jnp.minimum(slot[i], slots - 1), : BX * DZ] / blurred[i] for i in (0, 1)]
        out = [backward_tile(zb, yb, view[i], ratio[i]) for i in (0, 1)]
        for i in (0, 1):
            s_ref[:, pl.ds(row[i], BX), :] = out[i]


def sweep_body(slots, meta, est, left, right, topc, tops, botc, bots, data, xf, xb, zf, zb, yf, yb,
               omidc, omidl, omidr, otopc, otops, obotc, obots, s_ref, order):
    forward_x(s_ref, xf, est, left, right, topc, tops, botc, bots)
    clear_absent(slots, meta, s_ref)

    def predict(view, cell, row):
        return forward_tile(s_ref, zf, yf, view, row)

    visit_pairs(slots, meta, order, s_ref, data, zb, yb, predict)
    backward_x(s_ref, xb, omidc, omidl, omidr, otopc, otops, obotc, obots)


def blur_body(est, left, right, topc, tops, botc, bots, xf, zf, yf, out, s_ref):
    forward_x(s_ref, xf, est, left, right, topc, tops, botc, bots)

    @pl.loop(0, V * BLK_DEV // 2)
    def _(k):
        view = k // (BLK_DEV // 2)
        cells = (2 * k, 2 * k + 1)
        results = [
            forward_tile(s_ref, zf, yf, view, pl.multiple_of(cell * BX, BX)) for cell in cells
        ]
        for cell, result in zip(cells, results):
            out[cell] = result


def spread_body(slots, meta, blurred, data, xb, zb, yb,
                omidc, omidl, omidr, otopc, otops, obotc, obots, s_ref, order):
    clear_absent(slots, meta, s_ref)

    def predict(view, cell, row):
        return blurred[jnp.minimum(cell, V * BLK_DEV - 1)]

    visit_pairs(slots, meta, order, s_ref, data, zb, yb, predict)
    backward_x(s_ref, xb, omidc, omidl, omidr, otopc, otops, obotc, obots)


def f32(*shape):
    return jax.ShapeDtypeStruct(shape, jnp.float32)


VM = pl.BlockSpec(memory_space=pltpu.VMEM)
SM = pl.BlockSpec(memory_space=pltpu.SMEM)
PIECES = (
    f32(DZ, DX, NY),
    f32(DZ, RX, NY),
    f32(DZ, RX, NY),
    f32(RZ, DX, NY),
    f32(RZ, 2 * RX, NY),
    f32(RZ, DX, NY),
    f32(RZ, 2 * RX, NY),
)


def params(mib):
    return pltpu.CompilerParams(vmem_limit_bytes=mib * MIB)


FIELD = pltpu.VMEM((EZ, ROWS + BX, NY), jnp.float32)


def sweep(meta, pieces, data, tables):
    slots = data.shape[0]
    xf, xb, zf, zb, yf, yb = tables
    return pl.pallas_call(
        functools.partial(sweep_body, slots),
        out_shape=PIECES,
        in_specs=[SM] + [VM] * 14,
        out_specs=[VM] * 7,
        scratch_shapes=[FIELD, pltpu.SMEM((slots + 1,), jnp.int32)],
        compiler_params=params(36),
        name="sweep",
    )(meta, *pieces, data, xf, xb, zf, zb, yf, yb)


def blur_all(pieces, tables):
    xf, xb, zf, zb, yf, yb = tables
    return pl.pallas_call(
        blur_body,
        out_shape=f32(V * BLK_DEV, BX * DZ, NY),
        in_specs=[VM] * 10,
        out_specs=VM,
        scratch_shapes=[FIELD],
        compiler_params=params(34),
        name="blur_all",
    )(*pieces, xf, zf, yf)


def spread_ratio(meta, blurred, data, tables):
    slots = data.shape[0]
    xf, xb, zf, zb, yf, yb = tables
    return pl.pallas_call(
        functools.partial(spread_body, slots),
        out_shape=PIECES,
        in_specs=[SM] + [VM] * 5,
        out_specs=[VM] * 7,
        scratch_shapes=[FIELD, pltpu.SMEM((slots + 1,), jnp.int32)],
        compiler_params=params(34),
        name="spread_ratio",
    )(meta, blurred, data, xb, zb, yb)


def place_body(owner, pair, shift, tiles, out, staged, labels, sem, label_sem):
    count = tiles.shape[0]
    slots = out.shape[0]
    lane = lax.broadcasted_iota(jnp.int32, (8, NY), 1)
    values = jnp.zeros((8, NY), jnp.int32)
    for k in range(count):
        values = jnp.where(lane == k, pair[k], values)
        values = jnp.where(lane == count + k, shift[k], values)
    labels[...] = values.astype(jnp.float32)
    copies = []
    for slot in range(slots):
        copies.append(
            pltpu.make_async_copy(
                labels, out.at[slot, pl.ds(BX * DZ, 8)], label_sem.at[slot]
            )
        )
        copies[-1].start()
    column = lax.broadcasted_iota(jnp.int32, (DZ, BX, NY), 2)
    for k in range(count):
        moved = pltpu.roll(tiles[k], (shift[k] + NY) % NY, 2)
        source = column - shift[k]
        moved = jnp.where((source >= 0) & (source < NY), moved, 0.0)
        staged[k] = jnp.swapaxes(moved, 0, 1).reshape(BX * DZ, NY)
        copies.append(
            pltpu.make_async_copy(staged.at[k], out.at[owner[k], pl.ds(0, BX * DZ)], sem.at[k])
        )
        copies[-1].start()
    for copy in copies:
        copy.wait()


def place(owner, pair, shift, tiles, slots):
    count = tiles.shape[0]
    return pl.pallas_call(
        place_body,
        out_shape=f32(slots, BX * DZ + 8, NY),
        in_specs=[SM, SM, SM, VM],
        out_specs=pl.BlockSpec(memory_space=pltpu.HBM),
        scratch_shapes=[
            pltpu.VMEM((count, BX * DZ, NY), jnp.float32),
            pltpu.VMEM((8, NY), jnp.float32),
            pltpu.SemaphoreType.DMA((count,)),
            pltpu.SemaphoreType.DMA((slots,)),
        ],
        compiler_params=params(32),
        name="place",
    )(owner, pair, shift, tiles)


def rims_body(midl, midr, above, below, outl, outr):
    for mid, out, at in ((midl, outl, 0), (midr, outr, RX)):
        cols = pl.ds(at, RX)
        out[:RZ] = mid[:RZ] + above[:, cols]
        out[RZ : DZ - RZ] = mid[RZ : DZ - RZ]
        out[DZ - RZ :] = mid[DZ - RZ :] + below[:, cols]


def fold_rims(midl, midr, above, below):
    return pl.pallas_call(
        rims_body,
        out_shape=(f32(DZ, RX, NY), f32(DZ, RX, NY)),
        in_specs=[VM] * 4,
        out_specs=[VM] * 2,
        compiler_params=pltpu.CompilerParams(vmem_limit_bytes=32 * MIB),
        name="fold_rims",
    )(midl, midr, above, below)


def update_body(wz, est, midc, above, below, froml, fromr, gain, *outs):
    def step(z, extra):
        total = midc[z]
        if extra is not None:
            total = total + extra
        total = total + jnp.concatenate([froml[z], fromr[z]], axis=0)
        weight = wz[0, z] * gain[0]
        for view in range(1, V):
            weight = weight + wz[view, z] * gain[view]
        return est[z] * total / jnp.maximum(weight, 1.0)

    def write(z, new):
        outs[0][z] = new
        if len(outs) > 1:
            outs[1][z] = new[:RX]
            outs[2][z] = new[RX:]

    @pl.loop(0, RZ)
    def _(z):
        new = step(z, above[z])
        write(z, new)
        if len(outs) > 1:
            outs[3][z] = new

    for z in range(RZ, DZ - RZ):
        write(z, step(z, None))

    @pl.loop(0, RZ)
    def _(k):
        new = step(k + DZ - RZ, below[k])
        write(k + DZ - RZ, new)
        if len(outs) > 1:
            outs[4][k] = new


def update(wz, est, midc, above, below, froml, fromr, gain, last):
    shapes = [f32(DZ, DX, NY)]
    if not last:
        shapes += [f32(DZ, RX, NY)] * 2 + [f32(RZ, DX, NY)] * 2
    return pl.pallas_call(
        update_body,
        out_shape=tuple(shapes),
        in_specs=[SM] + [VM] * 7,
        out_specs=[VM] * len(shapes),
        compiler_params=pltpu.CompilerParams(vmem_limit_bytes=32 * MIB),
        name="update",
    )(wz, est, midc, above, below, froml, fromr, gain)


def band(row, rows, first):
    table = jnp.broadcast_to(row, (rows, row.shape[1]))
    return pltpu.roll(table, first % row.shape[1], 1, stride=1, stride_axis=0)


def tables_body(kz, kx, ky, xf, xb, zf, zb, yf, yb, yt):
    for view in range(V):
        full = band(kz[view : view + 1], DZ, PZ - RZ)
        high, low = split(full)
        zf[view] = jnp.concatenate(
            [jnp.concatenate([high, high], axis=1), jnp.concatenate([low, low], axis=1)], axis=0
        )
        high, low = split(full.T)
        zb[view] = jnp.concatenate([high, high, low], axis=1)
        full = band(ky[view : view + 1], NY, -15)[:, :NY]
        yt[view] = full
        high, low = split(full)
        half = jnp.concatenate([high, low], axis=1)
        yb[view] = jnp.concatenate([half, half], axis=0)
        high, low = split(full.T)
        half = jnp.concatenate([high, low], axis=1)
        yf[view] = jnp.concatenate([half, half], axis=0)
    full = jnp.concatenate([band(kx[v : v + 1], DX, RX - 15) for v in range(V)], axis=0)
    high, low = split(full[:, :EX])
    xf[...] = jnp.concatenate([high, high, low], axis=1)
    high, low = split(full.T[:EX])
    both = jnp.concatenate([high, low], axis=0)
    xb[...] = jnp.concatenate([both, both], axis=1)


def make_tables(kernel_z, kernel_x, kernel_y):
    def bf16(*shape):
        return jax.ShapeDtypeStruct(shape, jnp.bfloat16)

    def padded(kernel, lanes):
        return jnp.pad(kernel, ((0, 8 - V), (0, lanes - kernel.shape[1])))

    return pl.pallas_call(
        tables_body,
        out_shape=(
            bf16(ROWS, 3 * EX),
            bf16(2 * EX, 2 * ROWS),
            bf16(V, 2 * DZ, 2 * EZ),
            bf16(V, EZ, 3 * DZ),
            bf16(V, 2 * NY, 2 * NY),
            bf16(V, 2 * NY, 2 * NY),
            f32(V, NY, NY),
        ),
        in_specs=[VM] * 3,
        out_specs=[VM] * 7,
        compiler_params=params(32),
        name="tables",
    )(padded(kernel_z, 128), padded(kernel_x, 128), padded(kernel_y, 256))


def send(value, axis, step):
    count = lax.axis_size(axis)
    if step > 0:
        pairs = [(i, i + 1) for i in range(count - 1)]
    else:
        pairs = [(i + 1, i) for i in range(count - 1)]
    return lax.ppermute(value, axis, pairs)


def halo_columns(coll, colr):
    return send(colr, "blocks", 1), send(coll, "blocks", -1)


def halo(est, left, right, planet, planeb):
    botc = send(planet, "depth", -1)
    topc = send(planeb, "depth", 1)
    sides_t = jnp.concatenate([left[:RZ], right[:RZ]], axis=1)
    sides_b = jnp.concatenate([left[DZ - RZ :], right[DZ - RZ :]], axis=1)
    bots = send(sides_t, "depth", -1)
    tops = send(sides_b, "depth", 1)
    return est, left, right, topc, tops, botc, bots


def weight_parts(pairs, shifts, kernel_z, kernel_x, kernel_y, yt, all_blocks):
    planes = lax.axis_size("depth") * DZ
    view = pairs // all_blocks
    block = pairs % all_blocks
    taps = jnp.arange(kernel_z.shape[1])[None, :]
    z = lax.axis_index("depth") * DZ + jnp.arange(DZ)[:, None]
    reached = ((z - taps + RZ >= 0) & (z - taps + RZ < planes)).astype(jnp.float32)
    wz = jnp.einsum("va,za->vz", kernel_z, reached, precision=exact_mode)
    hot = (view[:, None] == jnp.arange(V)[None, :]).astype(jnp.float32)
    x = lax.axis_index("blocks") * DX + jnp.arange(DX)
    lead = x[None, :, None] + 15 - BX * block[:, None, None] - jnp.arange(kernel_x.shape[1])[None, None, :]
    covers = ((lead >= 0) & (lead < BX)).astype(jnp.float32)
    along_x = jnp.einsum("txb,vb->vtx", covers, kernel_x, precision=exact_mode) * hot.T[:, :, None]
    y = jnp.arange(NY)
    inside = (y[None, :] >= shifts[:, None]) & (y[None, :] < NY + shifts[:, None])
    along_y = jnp.einsum("ty,vyc->vtc", inside.astype(jnp.float32), yt, precision=exact_mode)
    gain = jnp.einsum("vtx,vtc->vxc", along_x, along_y, precision=exact_mode)
    return wz, gain


def local(estimate0, tiles, psf_z, psf_x, psf_y, tile_pair, tile_shift):
    owners = lax.axis_size("blocks")
    all_blocks = BLK_DEV * owners
    me = lax.axis_index("blocks")
    kernel_z = psf_z / jnp.sum(psf_z, axis=1, keepdims=True)
    kernel_x = psf_x / jnp.sum(psf_x, axis=1, keepdims=True)
    kernel_y = psf_y / jnp.sum(psf_y, axis=1, keepdims=True)

    held = tile_pair % all_blocks // BLK_DEV
    est = estimate0
    left, right = halo_columns(est[:, :RX], est[:, DX - RX :])
    sent = place(held, tile_pair, tile_shift, tiles, owners)
    sent, left, right = lax.optimization_barrier((sent, left, right))
    got = lax.all_to_all(sent, "blocks", split_axis=0, concat_axis=0, tiled=True)
    *tables, yt = make_tables(kernel_z, kernel_x, kernel_y)

    count = tiles.shape[0]
    labels = got[:, BX * DZ, : 2 * count].astype(jnp.int32)
    pairs, shifts = labels[:, :count], labels[:, count:]
    mine = pairs % all_blocks // BLK_DEV == me
    live = jnp.max(mine.astype(jnp.int32), axis=1)
    got_pair = jnp.sum(jnp.where(mine, pairs, 0), axis=1)
    view = got_pair // all_blocks
    cell = jnp.where(live > 0, view * BLK_DEV + got_pair % all_blocks - me * BLK_DEV, V * BLK_DEV)
    hit = cell[None, :] == jnp.arange(V * BLK_DEV)[:, None]
    present = jnp.max(hit.astype(jnp.int32), axis=1)
    end = lambda value: jnp.full((1,), value, jnp.int32)
    meta = jnp.concatenate([live, end(0), view, end(0), cell, end(V * BLK_DEV), present])
    meta = meta.astype(jnp.int32)
    wz, gain = weight_parts(
        pairs.reshape(-1), shifts.reshape(-1), kernel_z, kernel_x, kernel_y, yt, all_blocks
    )

    planes = est[:RZ], est[DZ - RZ :]
    for iteration in range(ITERS):
        pieces = halo(est, left, right, *planes)
        if iteration == 0:
            spread = spread_ratio(meta, blur_all(pieces, tables), got, tables)
        else:
            spread = sweep(meta, pieces, got, tables)
        midc, midl, midr, topc, tops, botc, bots = spread
        below_s = send(tops, "depth", -1)
        above_s = send(bots, "depth", 1)
        below_c = send(topc, "depth", -1)
        above_c = send(botc, "depth", 1)
        rim_l, rim_r = fold_rims(midl, midr, above_s, below_s)
        fromr = send(rim_l, "blocks", -1)
        froml = send(rim_r, "blocks", 1)
        last = iteration == ITERS - 1
        new = update(wz, est, midc, above_c, below_c, froml, fromr, gain, last)
        est = new[0]
        if not last:
            left, right = halo_columns(new[1], new[2])
            planes = new[3:]
    return est


def solution(mesh):
    in_specs = (
        P("depth", "blocks", None),
        P("blocks", "depth", None, None),
        P(),
        P(),
        P(),
        P("blocks"),
        P("blocks"),
    )
    out_specs = P("depth", "blocks", None)
    return jax.shard_map(local, mesh=mesh, in_specs=in_specs, out_specs=out_specs, check_vma=False)
```

```python
import functools

import jax
import jax.numpy as jnp
from jax import lax
from jax.experimental import pallas as pl
from jax.experimental.pallas import tpu as pltpu
from jax.sharding import PartitionSpec as P

BLK_DEV = 4
BX = 8
OFF = 8
ITERS = 2
V = 6
NY = 128
DZ = 64
DX = 32
RZ = 30
PZ = 32
RX = 16
EZ = DZ + 2 * PZ
EX = DX + 2 * RX
ROWS = V * DX
MIB = 1 << 20

exact_mode = lax.Precision.HIGHEST


def split(value):
    high = value.astype(jnp.bfloat16)
    low = (value - high.astype(jnp.float32)).astype(jnp.bfloat16)
    return high, low


def mul(a, b):
    return jnp.dot(a, b, preferred_element_type=jnp.float32)


def pair_columns(value, rows):
    return value[:, : value.shape[1] // 2], value[:, value.shape[1] // 2 :]


def blur_x(xf, planes, store):
    both = jnp.concatenate(planes, axis=1)
    high, low = split(both)
    out = mul(xf, jnp.concatenate([high, low, high], axis=0))
    store(out[:, :NY], out[:, NY:])


def starts(par, first, last):
    even = jnp.where(par[1] == 0, last, first)
    return even, first + last - even


def forward_x(par, s_ref, xf_ref, est, colse, colso, cene, ceno, side, sido):
    zeros = jnp.zeros((2, ROWS, NY), jnp.float32)
    s_ref[0:2, :ROWS] = zeros
    s_ref[EZ - 2 : EZ, :ROWS] = zeros
    plain = par[0] == 0

    def put(base):
        def store(first, second):
            s_ref[base, :ROWS] = first
            s_ref[base + 1, :ROWS] = second

        return store

    def rim(centre, sides, start):
        @pl.loop(0, RZ // 6)
        def _(group):
            for u in range(3):
                at = 6 * group + 2 * u
                planes = []
                for z in (at, at + 1):
                    planes.append(
                        jnp.concatenate([sides[z, :RX], centre[z], sides[z, RX:]], axis=0)
                    )
                blur_x(xf_ref[...], planes, put(start + at))

    @pl.loop(0, DZ // 8)
    def _(group):
        for u in range(4):
            at = 8 * group + 2 * u
            planes = []
            for z in (at, at + 1):
                even, odd = colse[z], colso[z]
                left, right = jnp.where(plain, odd, even), jnp.where(plain, even, odd)
                planes.append(jnp.concatenate([left, est[z], right], axis=0))
            blur_x(xf_ref[...], planes, put(PZ + at))

    even, odd = starts(par, PZ - RZ, PZ + DZ)
    rim(cene, side, even)
    rim(ceno, sido, odd)


def halves(value):
    middle = value.shape[1] // 2
    return value[:, :middle], value[:, middle:]


def forward_tile(s_ref, zf_ref, yf_ref, view, row):
    field = jnp.swapaxes(s_ref[:, pl.ds(row, BX), :], 0, 1)
    parts = []
    for p in range(BX // 2):
        high, low = split(jnp.concatenate([field[2 * p], field[2 * p + 1]], axis=1))
        out = mul(zf_ref[view], jnp.concatenate([high, low], axis=0))
        parts += halves(out[:DZ] + out[DZ:])
    high, low = split(jnp.concatenate(parts, axis=0))
    first, second = halves(mul(jnp.concatenate([high, low], axis=1), yf_ref[view]))
    return first + second


def backward_tile(zb_ref, yb_ref, view, ratio):
    high, low = split(ratio)
    first, second = halves(mul(jnp.concatenate([high, low], axis=1), yb_ref[view]))
    out = first + second
    parts = []
    for p in range(BX // 2):
        at = 2 * p * DZ
        high, low = split(jnp.concatenate([out[at : at + DZ], out[at + DZ : at + 2 * DZ]], axis=1))
        parts += halves(mul(zb_ref[view], jnp.concatenate([high, low, high], axis=0)))
    return jnp.swapaxes(jnp.stack(parts, axis=0), 0, 1)


def backward_x(par, s_ref, xb_ref, midc, midl, midr, cene, ceno, side, sido):
    def spread_pair(base):
        both = jnp.concatenate([s_ref[base, :ROWS], s_ref[base + 1, :ROWS]], axis=1)
        high, low = split(both)
        out = mul(xb_ref[...], jnp.concatenate([high, low], axis=0))
        return halves(out[:EX] + out[EX:])

    def rim(centre, sides, start):
        @pl.loop(0, RZ // 6)
        def _(group):
            for u in range(3):
                at = 6 * group + 2 * u
                for i, plane in enumerate(spread_pair(start + at)):
                    sides[at + i] = jnp.concatenate([plane[:RX], plane[RX + DX :]], axis=0)
                    centre[at + i] = plane[RX : RX + DX]

    even, odd = starts(par, PZ - RZ, PZ + DZ)
    rim(cene, side, even)
    rim(ceno, sido, odd)

    @pl.loop(0, DZ // 8)
    def _(group):
        for u in range(4):
            at = 8 * group + 2 * u
            for i, plane in enumerate(spread_pair(PZ + at)):
                midl[at + i] = plane[:RX]
                midc[at + i] = plane[RX : RX + DX]
                midr[at + i] = plane[RX + DX :]


def compact(slots, meta, order):
    count = jnp.int32(0)
    for slot in range(slots):
        order[count] = slot
        count = count + meta[slot]
    order[count] = slots
    return count


def clear_absent(slots, meta, s_ref):
    @pl.loop(0, V * BLK_DEV)
    def _(cell):
        @pl.when(meta[3 * (slots + 1) + cell] == 0)
        def _():
            s_ref[:, pl.ds(pl.multiple_of(cell * BX, BX), BX), :] = jnp.zeros(
                (EZ, BX, NY), jnp.float32
            )


def fetches(slots, meta, order, moves):
    count = compact(slots, meta, order)

    @pl.loop(0, count)
    def _(k):
        slot = order[k]
        for make in moves:
            make(slot, meta[2 * (slots + 1) + slot]).start()

    def arrive(slot):
        @pl.when(slot < slots)
        def _():
            for make in moves:
                make(slot, meta[2 * (slots + 1) + slot]).wait()

    return count, arrive


def visit_pairs(slots, meta, order, count, arrive, s_ref, data, zb, yb, predict):
    @pl.loop(0, (count + 1) // 2)
    def _(k):
        slot = (order[2 * k], order[2 * k + 1])
        for i in slot:
            arrive(i)
        view = [meta[slots + 1 + i] for i in slot]
        cell = [meta[2 * (slots + 1) + i] for i in slot]
        row = [pl.multiple_of(i * BX, BX) for i in cell]
        blurred = [predict(slot[i], view[i], row[i]) for i in (0, 1)]
        ratio = [data[slot[i]] / blurred[i] for i in (0, 1)]
        out = [backward_tile(zb, yb, view[i], ratio[i]) for i in (0, 1)]
        for i in (0, 1):
            s_ref[:, pl.ds(row[i], BX), :] = out[i]


def data_move(got, data, sem):
    def make(slot, cell):
        return pltpu.make_async_copy(
            got.at[slot, pl.ds(0, BX * DZ)], data.at[slot], sem.at[slot]
        )

    return make


def sweep_body(slots, par, meta, est, colse, colso, cene, ceno, side, sido, got, xf, xb, zf, zb, yf,
               yb, omidc, omidl, omidr, ocene, oceno, oside, osido, s_ref, order, data, sem):
    count, arrive = fetches(slots, meta, order, [data_move(got, data, sem)])
    forward_x(par, s_ref, xf, est, colse, colso, cene, ceno, side, sido)
    clear_absent(slots, meta, s_ref)

    def predict(slot, view, row):
        return forward_tile(s_ref, zf, yf, view, row)

    visit_pairs(slots, meta, order, count, arrive, s_ref, data, zb, yb, predict)
    backward_x(par, s_ref, xb, omidc, omidl, omidr, ocene, oceno, oside, osido)


def blur_body(par, est, colse, colso, cene, ceno, side, sido, xf, zf, yf, out, s_ref, staged, sem):
    forward_x(par, s_ref, xf, est, colse, colso, cene, ceno, side, sido)

    def push(k):
        return pltpu.make_async_copy(
            staged.at[pl.ds(2 * k, 2)], out.at[pl.ds(2 * k, 2)], sem.at[k]
        )

    @pl.loop(0, V * BLK_DEV // 2)
    def _(k):
        view = k // (BLK_DEV // 2)
        cells = (2 * k, 2 * k + 1)
        results = [
            forward_tile(s_ref, zf, yf, view, pl.multiple_of(cell * BX, BX)) for cell in cells
        ]
        for cell, result in zip(cells, results):
            staged[cell] = result
        push(k).start()

    @pl.loop(0, V * BLK_DEV // 2)
    def _(k):
        push(k).wait()


def spread_body(slots, par, meta, blurred, got, xb, zb, yb,
                omidc, omidl, omidr, ocene, oceno, oside, osido, s_ref, order, data, sem, held,
                held_sem):
    def make(slot, cell):
        return pltpu.make_async_copy(blurred.at[cell], held.at[slot], held_sem.at[slot])

    count, arrive = fetches(slots, meta, order, [make, data_move(got, data, sem)])
    clear_absent(slots, meta, s_ref)

    def predict(slot, view, row):
        return held[slot]

    visit_pairs(slots, meta, order, count, arrive, s_ref, data, zb, yb, predict)
    backward_x(par, s_ref, xb, omidc, omidl, omidr, ocene, oceno, oside, osido)


def f32(*shape):
    return jax.ShapeDtypeStruct(shape, jnp.float32)


VM = pl.BlockSpec(memory_space=pltpu.VMEM)
SM = pl.BlockSpec(memory_space=pltpu.SMEM)
PIECES = (
    f32(DZ, DX, NY),
    f32(DZ, RX, NY),
    f32(DZ, RX, NY),
    f32(RZ, DX, NY),
    f32(RZ, DX, NY),
    f32(RZ, 2 * RX, NY),
    f32(RZ, 2 * RX, NY),
)


def params(mib):
    return pltpu.CompilerParams(vmem_limit_bytes=mib * MIB)


FIELD = pltpu.VMEM((EZ, ROWS + BX, NY), jnp.float32)


def visit_scratch(slots):
    return [
        FIELD,
        pltpu.SMEM((slots + 1,), jnp.int32),
        pltpu.VMEM((slots + 1, BX * DZ, NY), jnp.float32),
        pltpu.SemaphoreType.DMA((slots + 1,)),
    ]


HB = pl.BlockSpec(memory_space=pltpu.HBM)


def in_hbm(value):
    return pltpu.with_memory_space_constraint(value, pltpu.HBM)


def sweep(par, meta, pieces, got, tables):
    slots = got.shape[0]
    return pl.pallas_call(
        functools.partial(sweep_body, slots),
        out_shape=PIECES,
        in_specs=[SM] * 2 + [VM] * 7 + [HB] + [VM] * 6,
        out_specs=[VM] * 7,
        scratch_shapes=visit_scratch(slots),
        compiler_params=params(36),
        name="sweep",
    )(par, meta, *pieces, in_hbm(got), *tables)


def blur_all(par, pieces, tables):
    xf, xb, zf, zb, yf, yb = tables
    cells = V * BLK_DEV
    return pl.pallas_call(
        blur_body,
        out_shape=pltpu.HBM((cells, BX * DZ, NY), jnp.float32),
        in_specs=[SM] + [VM] * 10,
        out_specs=HB,
        scratch_shapes=[
            FIELD,
            pltpu.VMEM((cells, BX * DZ, NY), jnp.float32),
            pltpu.SemaphoreType.DMA((cells // 2,)),
        ],
        compiler_params=params(34),
        name="blur_all",
    )(par, *pieces, xf, zf, yf)


def spread_ratio(par, meta, blurred, got, tables):
    slots = got.shape[0]
    xf, xb, zf, zb, yf, yb = tables
    return pl.pallas_call(
        functools.partial(spread_body, slots),
        out_shape=PIECES,
        in_specs=[SM] * 2 + [HB] * 2 + [VM] * 3,
        out_specs=[VM] * 7,
        scratch_shapes=visit_scratch(slots)
        + [
            pltpu.VMEM((slots + 1, BX * DZ, NY), jnp.float32),
            pltpu.SemaphoreType.DMA((slots + 1,)),
        ],
        compiler_params=params(36),
        name="spread_ratio",
    )(par, meta, in_hbm(blurred), in_hbm(got), xb, zb, yb)


def place_body(owner, pair, shift, tiles, out, staged, labels, sem, label_sem):
    count = tiles.shape[0]
    slots = out.shape[0]
    lane = lax.broadcasted_iota(jnp.int32, (8, NY), 1)
    values = jnp.zeros((8, NY), jnp.int32)
    for k in range(count):
        values = jnp.where(lane == k, pair[k], values)
        values = jnp.where(lane == count + k, shift[k], values)
    labels[...] = values.astype(jnp.float32)
    copies = []
    for slot in range(slots):
        copies.append(
            pltpu.make_async_copy(
                labels, out.at[slot, pl.ds(BX * DZ, 8)], label_sem.at[slot]
            )
        )
        copies[-1].start()
    column = lax.broadcasted_iota(jnp.int32, (DZ, BX, NY), 2)
    for k in range(count):
        moved = pltpu.roll(tiles[k], (shift[k] + NY) % NY, 2)
        source = column - shift[k]
        moved = jnp.where((source >= 0) & (source < NY), moved, 0.0)
        staged[k] = jnp.swapaxes(moved, 0, 1).reshape(BX * DZ, NY)
        copies.append(
            pltpu.make_async_copy(staged.at[k], out.at[owner[k], pl.ds(0, BX * DZ)], sem.at[k])
        )
        copies[-1].start()
    for copy in copies:
        copy.wait()


def place(owner, pair, shift, tiles, slots):
    count = tiles.shape[0]
    return pl.pallas_call(
        place_body,
        out_shape=pltpu.HBM((slots, BX * DZ + 8, NY), jnp.float32),
        in_specs=[SM, SM, SM, VM],
        out_specs=HB,
        scratch_shapes=[
            pltpu.VMEM((count, BX * DZ, NY), jnp.float32),
            pltpu.VMEM((8, NY), jnp.float32),
            pltpu.SemaphoreType.DMA((count,)),
            pltpu.SemaphoreType.DMA((slots,)),
        ],
        compiler_params=params(32),
        name="place",
    )(owner, pair, shift, tiles)


def pick(par, even_if_plain, other):
    plain = par[0] == 0
    return jnp.where(plain, even_if_plain, other), jnp.where(plain, other, even_if_plain)


def first_body(par, est, colse, colso, cene, ceno):
    @pl.loop(0, DZ // 4)
    def _(group):
        for u in range(4):
            z = 4 * group + u
            colse[z], colso[z] = pick(par, est[z, RX:], est[z, :RX])

    even, odd = starts(par, 0, DZ - RZ)

    @pl.loop(0, RZ // 6)
    def _(group):
        for u in range(6):
            k = 6 * group + u
            cene[k] = est[even + k]
            ceno[k] = est[odd + k]


COLUMNS = f32(DZ, RX, NY)
PLANES = f32(RZ, DX, NY)


def first_rims(par, est):
    return pl.pallas_call(
        first_body,
        out_shape=(COLUMNS, COLUMNS, PLANES, PLANES),
        in_specs=[SM, VM],
        out_specs=[VM] * 4,
        compiler_params=params(16),
        name="first_rims",
    )(par, est)


def rims_body(par, midl, midr, side, sido, outl, outr):
    even, odd = starts(par, 0, DZ - RZ)

    @pl.loop(0, DZ // 4)
    def _(group):
        for u in range(4):
            z = 4 * group + u
            outl[z], outr[z] = pick(par, midr[z], midl[z])

    for start, sides in ((even, side), (odd, sido)):

        @pl.loop(0, RZ // 6)
        def _(group):
            for u in range(6):
                k = 6 * group + u
                add, other = pick(par, sides[k, RX:], sides[k, :RX])
                outl[start + k] += add
                outr[start + k] += other


def fold_rims(par, midl, midr, side, sido):
    return pl.pallas_call(
        rims_body,
        out_shape=(COLUMNS, COLUMNS),
        in_specs=[SM] + [VM] * 4,
        out_specs=[VM] * 2,
        compiler_params=params(16),
        name="fold_rims",
    )(par, midl, midr, side, sido)


def corner_body(par, colse, colso, side, sido):
    even, odd = starts(par, 0, DZ - RZ)
    for start, out in ((even, side), (odd, sido)):

        @pl.loop(0, RZ // 6)
        def _(group):
            for u in range(6):
                k = 6 * group + u
                right, left = pick(par, colse[start + k], colso[start + k])
                out[k] = jnp.concatenate([left, right], axis=0)


def corners(par, colse, colso):
    return pl.pallas_call(
        corner_body,
        out_shape=(PLANES, PLANES),
        in_specs=[SM] + [VM] * 2,
        out_specs=[VM] * 2,
        compiler_params=params(16),
        name="corners",
    )(par, colse, colso)


def weigh_body(planes, blocks, at, labels, kz, kx, yb, out, along_x, inside, views):
    held = labels.shape[1] // 2
    lane = lax.broadcasted_iota(jnp.int32, (1, NY), 1)
    boxes = kx[...]
    for i in range(1, BX):
        boxes = boxes + pltpu.roll(kx[...], i, 1)
    along_x[...] = jnp.zeros(along_x.shape, jnp.float32)
    inside[...] = jnp.zeros(inside.shape, jnp.float32)
    views[...] = jnp.full(views.shape, -1, jnp.int32)

    @pl.loop(0, labels.shape[0])
    def _(holder):
        for k in range(held):
            pair = labels[holder, k]
            shift = labels[holder, held + k]
            view = pair // blocks
            beside = pair % blocks - at[0] * BLK_DEV

            @pl.when((beside >= -2) & (beside < BLK_DEV + 2))
            def _():
                row = holder * held + k
                box = jnp.zeros((1, NY), jnp.float32)
                for v in range(V):
                    box = jnp.where(view == v, boxes[v : v + 1], box)
                step = (BX * beside - 15 + NY) % NY
                moved = pltpu.roll(jnp.broadcast_to(box, (8, NY)), step, 1)
                along_x[pl.ds(row, 1), :] = moved[:1]
                seen = (lane >= shift) & (lane < NY + shift)
                inside[pl.ds(row, 1), :] = jnp.where(seen, 1.0, 0.0)
                views[pl.ds(row, 1), :] = jnp.full((1, NY), view, jnp.int32)

    z = at[1] * DZ + lax.broadcasted_iota(jnp.int32, (DZ, NY), 0)
    tap = lax.broadcasted_iota(jnp.int32, (DZ, NY), 1)
    reached = (z - tap + RZ >= 0) & (z - tap + RZ < planes)
    seen = inside[...].astype(jnp.bfloat16)
    gains, slopes = [], []
    for v in range(V):
        first, second = halves(mul(seen, yb[v, :NY]))
        member = jnp.where(views[...] == v, along_x[...], 0.0)
        gains.append(
            lax.dot_general(
                member.T[:DX],
                first + second,
                (((1,), (0,)), ((), ())),
                precision=exact_mode,
                preferred_element_type=jnp.float32,
            )
        )
        row = jnp.where(reached, jnp.broadcast_to(kz[v : v + 1], (DZ, NY)), 0.0)
        slopes.append(jnp.broadcast_to(jnp.sum(row, axis=1, keepdims=True), (DZ, NY)))
    for i in range(DZ):
        total = slopes[0][i : i + 1] * gains[0]
        for v in range(1, V):
            total = total + slopes[v][i : i + 1] * gains[v]
        out[i] = jnp.maximum(total, 1.0)


def weigh(planes, blocks, at, labels, kz, kx, yb):
    count = labels.shape[0] * labels.shape[1] // 2
    return pl.pallas_call(
        functools.partial(weigh_body, planes, blocks),
        out_shape=f32(DZ, DX, NY),
        in_specs=[SM] * 2 + [VM] * 3,
        out_specs=VM,
        scratch_shapes=[
            pltpu.VMEM((count, NY), jnp.float32),
            pltpu.VMEM((count, NY), jnp.float32),
            pltpu.VMEM((count, NY), jnp.int32),
        ],
        compiler_params=params(16),
        name="weigh",
    )(at, labels, kz, kx, yb)


def update_body(par, est, weight, midc, cene, ceno, colse, colso, new, *outs):
    even, odd = starts(par, 0, DZ - RZ)

    @pl.loop(0, DZ // 4)
    def _(group):
        for u in range(4):
            z = 4 * group + u
            right, left = pick(par, colse[z], colso[z])
            new[z] = midc[z] + jnp.concatenate([left, right], axis=0)

    for start, centre in ((even, cene), (odd, ceno)):

        @pl.loop(0, RZ // 6)
        def _(group):
            for u in range(6):
                new[start + 6 * group + u] += centre[6 * group + u]

    @pl.loop(0, DZ // 4)
    def _(group):
        for u in range(4):
            z = 4 * group + u
            value = est[z] * new[z] / weight[z]
            new[z] = value
            if outs:
                outs[0][z], outs[1][z] = pick(par, value[RX:], value[:RX])

    if outs:

        @pl.loop(0, RZ // 6)
        def _(group):
            for u in range(6):
                k = 6 * group + u
                outs[2][k] = new[even + k]
                outs[3][k] = new[odd + k]


def update(par, est, weight, midc, cene, ceno, colse, colso, last):
    shapes = [f32(DZ, DX, NY)]
    if not last:
        shapes += [COLUMNS, COLUMNS, PLANES, PLANES]
    return pl.pallas_call(
        update_body,
        out_shape=tuple(shapes),
        in_specs=[SM] + [VM] * 7,
        out_specs=[VM] * len(shapes),
        compiler_params=params(16),
        name="update",
    )(par, est, weight, midc, cene, ceno, colse, colso)


def band(row, rows, first):
    table = jnp.broadcast_to(row, (rows, row.shape[1]))
    return pltpu.roll(table, first % row.shape[1], 1, stride=1, stride_axis=0)


def tables_body(kz, kx, ky, xf, xb, zf, zb, yf, yb):
    for view in range(V):
        full = band(kz[view : view + 1], DZ, PZ - RZ)
        high, low = split(full)
        zf[view] = jnp.concatenate(
            [jnp.concatenate([high, high], axis=1), jnp.concatenate([low, low], axis=1)], axis=0
        )
        high, low = split(full.T)
        zb[view] = jnp.concatenate([high, high, low], axis=1)
        full = band(ky[view : view + 1], NY, -15)[:, :NY]
        high, low = split(full)
        half = jnp.concatenate([high, low], axis=1)
        yb[view] = jnp.concatenate([half, half], axis=0)
        high, low = split(full.T)
        half = jnp.concatenate([high, low], axis=1)
        yf[view] = jnp.concatenate([half, half], axis=0)
    full = jnp.concatenate([band(kx[v : v + 1], DX, RX - 15) for v in range(V)], axis=0)
    high, low = split(full[:, :EX])
    xf[...] = jnp.concatenate([high, high, low], axis=1)
    high, low = split(full.T[:EX])
    both = jnp.concatenate([high, low], axis=0)
    xb[...] = jnp.concatenate([both, both], axis=1)


def padded(kernel, lanes):
    return jnp.pad(kernel, ((0, 8 - V), (0, lanes - kernel.shape[1])))


def make_tables(kernel_z, kernel_x, kernel_y):
    def bf16(*shape):
        return jax.ShapeDtypeStruct(shape, jnp.bfloat16)

    return pl.pallas_call(
        tables_body,
        out_shape=(
            bf16(ROWS, 3 * EX),
            bf16(2 * EX, 2 * ROWS),
            bf16(V, 2 * DZ, 2 * EZ),
            bf16(V, EZ, 3 * DZ),
            bf16(V, 2 * NY, 2 * NY),
            bf16(V, 2 * NY, 2 * NY),
        ),
        in_specs=[VM] * 3,
        out_specs=[VM] * 6,
        compiler_params=params(32),
        name="tables",
    )(kernel_z, kernel_x, kernel_y)


def swap(even, odd, axis):
    count = lax.axis_size(axis)
    out = []
    for value, first in ((even, 0), (odd, 1)):
        pairs = []
        for i in range(first, count - 1, 2):
            pairs += [(i, i + 1), (i + 1, i)]
        out.append(lax.ppermute(value, axis, pairs))
    return out


def local(estimate0, tiles, psf_z, psf_x, psf_y, tile_pair, tile_shift):
    owners = lax.axis_size("blocks")
    all_blocks = BLK_DEV * owners
    me = lax.axis_index("blocks")
    kernel_z = padded(psf_z / jnp.sum(psf_z, axis=1, keepdims=True), 128)
    kernel_x = padded(psf_x / jnp.sum(psf_x, axis=1, keepdims=True), 128)
    kernel_y = padded(psf_y / jnp.sum(psf_y, axis=1, keepdims=True), 256)

    held = tile_pair % all_blocks // BLK_DEV
    est = estimate0
    par = jnp.stack([me % 2, lax.axis_index("depth") % 2]).astype(jnp.int32)
    *columns, cene, ceno = first_rims(par, est)
    columns = swap(*columns, "blocks")
    sent = place(held, tile_pair, tile_shift, tiles, owners)
    sent, *columns = lax.optimization_barrier((sent, *columns))
    got = lax.all_to_all(sent, "blocks", split_axis=0, concat_axis=0, tiled=True)
    tables = make_tables(kernel_z, kernel_x, kernel_y)

    count = tiles.shape[0]
    labels = got[:, BX * DZ, : 2 * count].astype(jnp.int32)
    pairs, shifts = labels[:, :count], labels[:, count:]
    mine = pairs % all_blocks // BLK_DEV == me
    live = jnp.max(mine.astype(jnp.int32), axis=1)
    got_pair = jnp.sum(jnp.where(mine, pairs, 0), axis=1)
    view = got_pair // all_blocks
    cell = jnp.where(live > 0, view * BLK_DEV + got_pair % all_blocks - me * BLK_DEV, V * BLK_DEV)
    hit = cell[None, :] == jnp.arange(V * BLK_DEV)[:, None]
    present = jnp.max(hit.astype(jnp.int32), axis=1)
    end = lambda value: jnp.full((1,), value, jnp.int32)
    meta = jnp.concatenate([live, end(0), view, end(0), cell, end(V * BLK_DEV), present])
    meta = meta.astype(jnp.int32)
    at = jnp.stack([me, lax.axis_index("depth")]).astype(jnp.int32)
    planes = lax.axis_size("depth") * DZ
    weight = weigh(planes, all_blocks, at, labels, kernel_z, kernel_x, tables[5])

    for iteration in range(ITERS):
        centre = swap(cene, ceno, "depth")
        sides = swap(*corners(par, *columns), "depth")
        pieces = (est, *columns, *centre, *sides)
        if iteration == 0:
            spread = spread_ratio(par, meta, blur_all(par, pieces, tables), got, tables)
        else:
            spread = sweep(par, meta, pieces, got, tables)
        midc, midl, midr, cene, ceno, side, sido = spread
        side, sido = swap(side, sido, "depth")
        rims = fold_rims(par, midl, midr, side, sido)
        cene, ceno, *rims = lax.optimization_barrier((cene, ceno, *rims))
        columns = swap(*rims, "blocks")
        cene, ceno = swap(cene, ceno, "depth")
        last = iteration == ITERS - 1
        est, *rest = update(par, est, weight, midc, cene, ceno, *columns, last)
        if not last:
            *columns, cene, ceno = rest
            columns = swap(*columns, "blocks")
    return est


def solution(mesh):
    in_specs = (
        P("depth", "blocks", None),
        P("blocks", "depth", None, None),
        P(),
        P(),
        P(),
        P("blocks"),
        P("blocks"),
    )
    out_specs = P("depth", "blocks", None)
    return jax.shard_map(local, mesh=mesh, in_specs=in_specs, out_specs=out_specs, check_vma=False)
```

```python
import functools

import jax
import jax.numpy as jnp
from jax import lax
from jax.experimental import pallas as pl
from jax.experimental.pallas import tpu as pltpu
from jax.sharding import PartitionSpec as P

BLK_DEV = 4
BX = 8
OFF = 8
ITERS = 2
V = 6
NY = 128
DZ = 64
DX = 32
RZ = 30
PZ = 32
RX = 16
EZ = DZ + 2 * PZ
EX = DX + 2 * RX
ROWS = V * DX
MIB = 1 << 20

exact_mode = lax.Precision.HIGHEST


def split(value):
    high = value.astype(jnp.bfloat16)
    low = (value - high.astype(jnp.float32)).astype(jnp.bfloat16)
    return high, low


def mul(a, b):
    return jnp.dot(a, b, preferred_element_type=jnp.float32)


def pair_columns(value, rows):
    return value[:, : value.shape[1] // 2], value[:, value.shape[1] // 2 :]


def blur_x(xf, planes, store):
    both = jnp.concatenate(planes, axis=1)
    high, low = split(both)
    out = mul(xf, jnp.concatenate([high, low, high], axis=0))
    store(out[:, :NY], out[:, NY:])


def starts(par, first, last):
    even = jnp.where(par[1] == 0, last, first)
    return even, first + last - even


def forward_x(par, s_ref, xf_ref, est, colse, colso, cene, ceno, side, sido):
    zeros = jnp.zeros((2,) + s_ref.shape[1:], jnp.float32)
    s_ref[0:2] = zeros
    s_ref[EZ - 2 : EZ] = zeros
    plain = par[0] == 0

    def put(base):
        def store(first, second):
            s_ref[base] = first
            s_ref[base + 1] = second

        return store

    def rim(centre, sides, start):
        @pl.loop(0, RZ // 30)
        def _(group):
            for u in range(15):
                at = 30 * group + 2 * u
                planes = []
                for z in (at, at + 1):
                    planes.append(
                        jnp.concatenate([sides[z, :RX], centre[z], sides[z, RX:]], axis=0)
                    )
                blur_x(xf_ref[...], planes, put(start + at))

    @pl.loop(0, DZ // 64)
    def _(group):
        for u in range(32):
            at = 64 * group + 2 * u
            planes = []
            for z in (at, at + 1):
                even, odd = colse[z], colso[z]
                left, right = jnp.where(plain, odd, even), jnp.where(plain, even, odd)
                planes.append(jnp.concatenate([left, est[z], right], axis=0))
            blur_x(xf_ref[...], planes, put(PZ + at))

    even, odd = starts(par, PZ - RZ, PZ + DZ)
    rim(cene, side, even)
    rim(ceno, sido, odd)


def halves(value):
    middle = value.shape[1] // 2
    return value[:, :middle], value[:, middle:]


def forward_tile(s_ref, zf_ref, yf_ref, view, row):
    field = jnp.swapaxes(s_ref[:, pl.ds(row, BX), :], 0, 1)
    parts = []
    for p in range(BX // 2):
        high, low = split(jnp.concatenate([field[2 * p], field[2 * p + 1]], axis=1))
        out = mul(zf_ref[view], jnp.concatenate([high, low], axis=0))
        parts += halves(out[:DZ] + out[DZ:])
    high, low = split(jnp.concatenate(parts, axis=0))
    first, second = halves(mul(jnp.concatenate([high, low], axis=1), yf_ref[view]))
    return first + second


def backward_tile(zb_ref, yb_ref, view, ratio):
    high, low = split(ratio)
    first, second = halves(mul(jnp.concatenate([high, low], axis=1), yb_ref[view]))
    out = first + second
    parts = []
    for p in range(BX // 2):
        at = 2 * p * DZ
        high, low = split(jnp.concatenate([out[at : at + DZ], out[at + DZ : at + 2 * DZ]], axis=1))
        parts += halves(mul(zb_ref[view], jnp.concatenate([high, low, high], axis=0)))
    return jnp.swapaxes(jnp.stack(parts, axis=0), 0, 1)


def backward_x(par, s_ref, xb_ref, midc, midl, midr, cene, ceno, side, sido):
    def spread_pair(base):
        both = jnp.concatenate([s_ref[base], s_ref[base + 1]], axis=1)
        high, low = split(both)
        out = mul(xb_ref[...], jnp.concatenate([high, low], axis=0))
        return halves(out[:EX] + out[EX:])

    def rim(centre, sides, start):
        @pl.loop(0, RZ // 30)
        def _(group):
            for u in range(15):
                at = 30 * group + 2 * u
                for i, plane in enumerate(spread_pair(start + at)):
                    sides[at + i] = jnp.concatenate([plane[:RX], plane[RX + DX :]], axis=0)
                    centre[at + i] = plane[RX : RX + DX]

    even, odd = starts(par, PZ - RZ, PZ + DZ)
    rim(cene, side, even)
    rim(ceno, sido, odd)

    @pl.loop(0, DZ // 64)
    def _(group):
        for u in range(32):
            at = 64 * group + 2 * u
            for i, plane in enumerate(spread_pair(PZ + at)):
                midl[at + i] = plane[:RX]
                midc[at + i] = plane[RX : RX + DX]
                midr[at + i] = plane[RX + DX :]


def compact(slots, meta, order):
    count = jnp.int32(0)
    for slot in range(slots):
        order[count] = slot
        count = count + meta[slot]
    order[count] = slots
    return count


def gather_x(slots, meta, order, count, fx, picked, xf, xb):
    for n in range(slots):
        slot = jnp.where(n < count, order[n], slots)
        cell = jnp.where(n < count, meta[2 * (slots + 1) + slot], 0)
        scale = jnp.where(n < count, 1.0, 0.0)
        picked[n * BX : (n + 1) * BX] = fx[cell] * scale
    table = picked[...]
    if xf is not None:
        high, low = split(table[:, :EX])
        xf[...] = jnp.concatenate([high, high, low], axis=1)
    high, low = split(table.T[:EX])
    both = jnp.concatenate([high, low], axis=0)
    xb[...] = jnp.concatenate([both, both], axis=1)


def clear_rest(slots, count, s_ref):
    @pl.loop(count, slots)
    def _(n):
        s_ref[:, pl.ds(pl.multiple_of(n * BX, BX), BX), :] = jnp.zeros((EZ, BX, NY), jnp.float32)


def fetches(slots, meta, order, moves):
    count = compact(slots, meta, order)

    @pl.loop(0, count)
    def _(k):
        slot = order[k]
        for make in moves:
            make(slot, meta[2 * (slots + 1) + slot]).start()

    def arrive(slot):
        @pl.when(slot < slots)
        def _():
            for make in moves:
                make(slot, meta[2 * (slots + 1) + slot]).wait()

    return count, arrive


def visit_tiles(step, slots, meta, order, count, arrive, s_ref, data, zb, yb, predict):
    @pl.loop(0, (count + step - 1) // step)
    def _(k):
        slot = [
            jnp.where(step * k + i < count, order[step * k + i], slots) for i in range(step)
        ]
        for i in slot:
            arrive(i)
        view = [meta[slots + 1 + i] for i in slot]
        row = [pl.multiple_of((step * k + i) * BX, BX) for i in range(step)]
        blurred = [predict(slot[i], view[i], row[i]) for i in range(step)]
        out = [
            backward_tile(zb, yb, view[i], data[slot[i]] / blurred[i]) for i in range(step)
        ]
        for i in range(step):
            s_ref[:, pl.ds(row[i], BX), :] = out[i]


def data_move(got, data, sem):
    def make(slot, cell):
        return pltpu.make_async_copy(
            got.at[slot, pl.ds(0, BX * DZ)], data.at[slot], sem.at[slot]
        )

    return make


def sweep_body(slots, par, meta, est, colse, colso, cene, ceno, side, sido, got, fx, zf, zb, yf,
               yb, omidc, omidl, omidr, ocene, oceno, oside, osido, s_ref, order, data, sem, picked,
               xb, xf):
    count, arrive = fetches(slots, meta, order, [data_move(got, data, sem)])
    gather_x(slots, meta, order, count, fx, picked, xf, xb)
    forward_x(par, s_ref, xf, est, colse, colso, cene, ceno, side, sido)

    def predict(slot, view, row):
        return forward_tile(s_ref, zf, yf, view, row)

    visit_tiles(2, slots, meta, order, count, arrive, s_ref, data, zb, yb, predict)
    clear_rest(slots, count, s_ref)
    backward_x(par, s_ref, xb, omidc, omidl, omidr, ocene, oceno, oside, osido)


def blur_body(par, est, colse, colso, cene, ceno, side, sido, xf, zf, yf, out, s_ref, staged, sem):
    forward_x(par, s_ref, xf, est, colse, colso, cene, ceno, side, sido)

    def push(k):
        return pltpu.make_async_copy(
            staged.at[pl.ds(2 * k, 2)], out.at[pl.ds(2 * k, 2)], sem.at[k]
        )

    @pl.loop(0, V * BLK_DEV // 2)
    def _(k):
        view = k // (BLK_DEV // 2)
        cells = (2 * k, 2 * k + 1)
        results = [
            forward_tile(s_ref, zf, yf, view, pl.multiple_of(cell * BX, BX)) for cell in cells
        ]
        for cell, result in zip(cells, results):
            staged[cell] = result
        push(k).start()

    @pl.loop(0, V * BLK_DEV // 2)
    def _(k):
        push(k).wait()


def spread_body(slots, par, meta, blurred, got, fx, zb, yb,
                omidc, omidl, omidr, ocene, oceno, oside, osido, s_ref, order, data, sem, picked,
                xb, held, held_sem):
    def make(slot, cell):
        return pltpu.make_async_copy(blurred.at[cell], held.at[slot], held_sem.at[slot])

    count, arrive = fetches(slots, meta, order, [make, data_move(got, data, sem)])
    gather_x(slots, meta, order, count, fx, picked, None, xb)

    def predict(slot, view, row):
        return held[slot]

    visit_tiles(4, slots, meta, order, count, arrive, s_ref, data, zb, yb, predict)
    clear_rest(slots, count, s_ref)
    backward_x(par, s_ref, xb, omidc, omidl, omidr, ocene, oceno, oside, osido)


def f32(*shape):
    return jax.ShapeDtypeStruct(shape, jnp.float32)


VM = pl.BlockSpec(memory_space=pltpu.VMEM)
SM = pl.BlockSpec(memory_space=pltpu.SMEM)
PIECES = (
    f32(DZ, DX, NY),
    f32(DZ, RX, NY),
    f32(DZ, RX, NY),
    f32(RZ, DX, NY),
    f32(RZ, DX, NY),
    f32(RZ, 2 * RX, NY),
    f32(RZ, 2 * RX, NY),
)


def params(mib):
    return pltpu.CompilerParams(vmem_limit_bytes=mib * MIB)


def visit_scratch(slots):
    rows = slots * BX
    return [
        pltpu.VMEM((EZ, rows, NY), jnp.float32),
        pltpu.SMEM((slots + 1,), jnp.int32),
        pltpu.VMEM((slots + 1, BX * DZ, NY), jnp.float32),
        pltpu.SemaphoreType.DMA((slots + 1,)),
        pltpu.VMEM((rows, NY), jnp.float32),
        pltpu.VMEM((2 * EX, 2 * rows), jnp.bfloat16),
    ]


HB = pl.BlockSpec(memory_space=pltpu.HBM)


def in_hbm(value):
    return pltpu.with_memory_space_constraint(value, pltpu.HBM)


def sweep(par, meta, pieces, got, tables):
    slots = got.shape[0]
    return pl.pallas_call(
        functools.partial(sweep_body, slots),
        out_shape=PIECES,
        in_specs=[SM] * 2 + [VM] * 7 + [HB] + [VM] * 5,
        out_specs=[VM] * 7,
        scratch_shapes=visit_scratch(slots) + [pltpu.VMEM((slots * BX, 3 * EX), jnp.bfloat16)],
        compiler_params=params(36),
        name="sweep",
    )(par, meta, *pieces, in_hbm(got), *tables[1:])


def blur_all(par, pieces, tables):
    xf, fx, zf, zb, yf, yb = tables
    cells = V * BLK_DEV
    return pl.pallas_call(
        blur_body,
        out_shape=pltpu.HBM((cells, BX * DZ, NY), jnp.float32),
        in_specs=[SM] + [VM] * 10,
        out_specs=HB,
        scratch_shapes=[
            pltpu.VMEM((EZ, ROWS, NY), jnp.float32),
            pltpu.VMEM((cells, BX * DZ, NY), jnp.float32),
            pltpu.SemaphoreType.DMA((cells // 2,)),
        ],
        compiler_params=params(34),
        name="blur_all",
    )(par, *pieces, xf, zf, yf)


def spread_ratio(par, meta, blurred, got, tables):
    slots = got.shape[0]
    xf, fx, zf, zb, yf, yb = tables
    return pl.pallas_call(
        functools.partial(spread_body, slots),
        out_shape=PIECES,
        in_specs=[SM] * 2 + [HB] * 2 + [VM] * 3,
        out_specs=[VM] * 7,
        scratch_shapes=visit_scratch(slots)
        + [
            pltpu.VMEM((slots + 1, BX * DZ, NY), jnp.float32),
            pltpu.SemaphoreType.DMA((slots + 1,)),
        ],
        compiler_params=params(36),
        name="spread_ratio",
    )(par, meta, in_hbm(blurred), in_hbm(got), fx, zb, yb)


def place_body(owner, pair, shift, tiles, out, staged, labels, sem, label_sem):
    count = tiles.shape[0]
    slots = out.shape[0]
    lane = lax.broadcasted_iota(jnp.int32, (8, NY), 1)
    values = jnp.zeros((8, NY), jnp.int32)
    for k in range(count):
        values = jnp.where(lane == k, pair[k], values)
        values = jnp.where(lane == count + k, shift[k], values)
    labels[...] = values.astype(jnp.float32)
    copies = []
    for slot in range(slots):
        copies.append(
            pltpu.make_async_copy(
                labels, out.at[slot, pl.ds(BX * DZ, 8)], label_sem.at[slot]
            )
        )
        copies[-1].start()
    column = lax.broadcasted_iota(jnp.int32, (DZ, BX, NY), 2)
    for k in range(count):
        moved = pltpu.roll(tiles[k], (shift[k] + NY) % NY, 2)
        source = column - shift[k]
        moved = jnp.where((source >= 0) & (source < NY), moved, 0.0)
        staged[k] = jnp.swapaxes(moved, 0, 1).reshape(BX * DZ, NY)
        copies.append(
            pltpu.make_async_copy(staged.at[k], out.at[owner[k], pl.ds(0, BX * DZ)], sem.at[k])
        )
        copies[-1].start()
    for copy in copies:
        copy.wait()


def place(owner, pair, shift, tiles, slots):
    count = tiles.shape[0]
    return pl.pallas_call(
        place_body,
        out_shape=pltpu.HBM((slots, BX * DZ + 8, NY), jnp.float32),
        in_specs=[SM, SM, SM, VM],
        out_specs=HB,
        scratch_shapes=[
            pltpu.VMEM((count, BX * DZ, NY), jnp.float32),
            pltpu.VMEM((8, NY), jnp.float32),
            pltpu.SemaphoreType.DMA((count,)),
            pltpu.SemaphoreType.DMA((slots,)),
        ],
        compiler_params=params(32),
        name="place",
    )(owner, pair, shift, tiles)


def pick(par, even_if_plain, other):
    plain = par[0] == 0
    return jnp.where(plain, even_if_plain, other), jnp.where(plain, other, even_if_plain)


def first_body(par, est, colse, colso, cene, ceno):
    @pl.loop(0, DZ // 4)
    def _(group):
        for u in range(4):
            z = 4 * group + u
            colse[z], colso[z] = pick(par, est[z, RX:], est[z, :RX])

    even, odd = starts(par, 0, DZ - RZ)

    @pl.loop(0, RZ // 6)
    def _(group):
        for u in range(6):
            k = 6 * group + u
            cene[k] = est[even + k]
            ceno[k] = est[odd + k]


COLUMNS = f32(DZ, RX, NY)
PLANES = f32(RZ, DX, NY)


def first_rims(par, est):
    return pl.pallas_call(
        first_body,
        out_shape=(COLUMNS, COLUMNS, PLANES, PLANES),
        in_specs=[SM, VM],
        out_specs=[VM] * 4,
        compiler_params=params(16),
        name="first_rims",
    )(par, est)


def rims_body(par, midl, midr, side, sido, outl, outr):
    even, odd = starts(par, 0, DZ - RZ)

    @pl.loop(0, DZ // 4)
    def _(group):
        for u in range(4):
            z = 4 * group + u
            outl[z], outr[z] = pick(par, midr[z], midl[z])

    for start, sides in ((even, side), (odd, sido)):

        @pl.loop(0, RZ // 6)
        def _(group):
            for u in range(6):
                k = 6 * group + u
                add, other = pick(par, sides[k, RX:], sides[k, :RX])
                outl[start + k] += add
                outr[start + k] += other


def fold_rims(par, midl, midr, side, sido):
    return pl.pallas_call(
        rims_body,
        out_shape=(COLUMNS, COLUMNS),
        in_specs=[SM] + [VM] * 4,
        out_specs=[VM] * 2,
        compiler_params=params(16),
        name="fold_rims",
    )(par, midl, midr, side, sido)


def corner_body(par, colse, colso, side, sido):
    even, odd = starts(par, 0, DZ - RZ)
    for start, out in ((even, side), (odd, sido)):

        @pl.loop(0, RZ // 6)
        def _(group):
            for u in range(6):
                k = 6 * group + u
                right, left = pick(par, colse[start + k], colso[start + k])
                out[k] = jnp.concatenate([left, right], axis=0)


def corners(par, colse, colso):
    return pl.pallas_call(
        corner_body,
        out_shape=(PLANES, PLANES),
        in_specs=[SM] + [VM] * 2,
        out_specs=[VM] * 2,
        compiler_params=params(16),
        name="corners",
    )(par, colse, colso)


def weigh_body(planes, blocks, at, labels, kz, kx, yb, out, along_x, inside, views):
    held = labels.shape[1] // 2
    lane = lax.broadcasted_iota(jnp.int32, (1, NY), 1)
    boxes = kx[...]
    for i in range(1, BX):
        boxes = boxes + pltpu.roll(kx[...], i, 1)
    along_x[...] = jnp.zeros(along_x.shape, jnp.float32)
    inside[...] = jnp.zeros(inside.shape, jnp.float32)
    views[...] = jnp.full(views.shape, -1, jnp.int32)

    @pl.loop(0, labels.shape[0])
    def _(holder):
        for k in range(held):
            pair = labels[holder, k]
            shift = labels[holder, held + k]
            view = pair // blocks
            beside = pair % blocks - at[0] * BLK_DEV

            @pl.when((beside >= -2) & (beside < BLK_DEV + 2))
            def _():
                row = holder * held + k
                box = jnp.zeros((1, NY), jnp.float32)
                for v in range(V):
                    box = jnp.where(view == v, boxes[v : v + 1], box)
                step = (BX * beside - 15 + NY) % NY
                moved = pltpu.roll(jnp.broadcast_to(box, (8, NY)), step, 1)
                along_x[pl.ds(row, 1), :] = moved[:1]
                seen = (lane >= shift) & (lane < NY + shift)
                inside[pl.ds(row, 1), :] = jnp.where(seen, 1.0, 0.0)
                views[pl.ds(row, 1), :] = jnp.full((1, NY), view, jnp.int32)

    z = at[1] * DZ + lax.broadcasted_iota(jnp.int32, (DZ, NY), 0)
    tap = lax.broadcasted_iota(jnp.int32, (DZ, NY), 1)
    reached = (z - tap + RZ >= 0) & (z - tap + RZ < planes)
    seen = inside[...].astype(jnp.bfloat16)
    gains, slopes = [], []
    for v in range(V):
        first, second = halves(mul(seen, yb[v, :NY]))
        member = jnp.where(views[...] == v, along_x[...], 0.0)
        gains.append(
            lax.dot_general(
                member.T[:DX],
                first + second,
                (((1,), (0,)), ((), ())),
                precision=exact_mode,
                preferred_element_type=jnp.float32,
            )
        )
        row = jnp.where(reached, jnp.broadcast_to(kz[v : v + 1], (DZ, NY)), 0.0)
        slopes.append(jnp.broadcast_to(jnp.sum(row, axis=1, keepdims=True), (DZ, NY)))
    for i in range(DZ):
        total = slopes[0][i : i + 1] * gains[0]
        for v in range(1, V):
            total = total + slopes[v][i : i + 1] * gains[v]
        out[i] = jnp.maximum(total, 1.0)


def weigh(planes, blocks, at, labels, kz, kx, yb):
    count = labels.shape[0] * labels.shape[1] // 2
    return pl.pallas_call(
        functools.partial(weigh_body, planes, blocks),
        out_shape=f32(DZ, DX, NY),
        in_specs=[SM] * 2 + [VM] * 3,
        out_specs=VM,
        scratch_shapes=[
            pltpu.VMEM((count, NY), jnp.float32),
            pltpu.VMEM((count, NY), jnp.float32),
            pltpu.VMEM((count, NY), jnp.int32),
        ],
        compiler_params=params(16),
        name="weigh",
    )(at, labels, kz, kx, yb)


def update_body(par, est, weight, midc, cene, ceno, colse, colso, new, *outs):
    even, odd = starts(par, 0, DZ - RZ)

    @pl.loop(0, DZ // 4)
    def _(group):
        for u in range(4):
            z = 4 * group + u
            right, left = pick(par, colse[z], colso[z])
            new[z] = midc[z] + jnp.concatenate([left, right], axis=0)

    for start, centre in ((even, cene), (odd, ceno)):

        @pl.loop(0, RZ // 6)
        def _(group):
            for u in range(6):
                new[start + 6 * group + u] += centre[6 * group + u]

    @pl.loop(0, DZ // 4)
    def _(group):
        for u in range(4):
            z = 4 * group + u
            value = est[z] * new[z] / weight[z]
            new[z] = value
            if outs:
                outs[0][z], outs[1][z] = pick(par, value[RX:], value[:RX])

    if outs:

        @pl.loop(0, RZ // 6)
        def _(group):
            for u in range(6):
                k = 6 * group + u
                outs[2][k] = new[even + k]
                outs[3][k] = new[odd + k]


def update(par, est, weight, midc, cene, ceno, colse, colso, last):
    shapes = [f32(DZ, DX, NY)]
    if not last:
        shapes += [COLUMNS, COLUMNS, PLANES, PLANES]
    return pl.pallas_call(
        update_body,
        out_shape=tuple(shapes),
        in_specs=[SM] + [VM] * 7,
        out_specs=[VM] * len(shapes),
        compiler_params=params(16),
        name="update",
    )(par, est, weight, midc, cene, ceno, colse, colso)


def band(row, rows, first):
    table = jnp.broadcast_to(row, (rows, row.shape[1]))
    return pltpu.roll(table, first % row.shape[1], 1, stride=1, stride_axis=0)


def tables_body(kz, kx, ky, xf, fx, zf, zb, yf, yb):
    for view in range(V):
        full = band(kz[view : view + 1], DZ, PZ - RZ)
        high, low = split(full)
        zf[view] = jnp.concatenate(
            [jnp.concatenate([high, high], axis=1), jnp.concatenate([low, low], axis=1)], axis=0
        )
        high, low = split(full.T)
        zb[view] = jnp.concatenate([high, high, low], axis=1)
        full = band(ky[view : view + 1], NY, -15)[:, :NY]
        high, low = split(full)
        half = jnp.concatenate([high, low], axis=1)
        yb[view] = jnp.concatenate([half, half], axis=0)
        high, low = split(full.T)
        half = jnp.concatenate([high, low], axis=1)
        yf[view] = jnp.concatenate([half, half], axis=0)
    full = jnp.concatenate([band(kx[v : v + 1], DX, RX - 15) for v in range(V)], axis=0)
    fx[...] = full.reshape(V * BLK_DEV, BX, NY)
    high, low = split(full[:, :EX])
    xf[...] = jnp.concatenate([high, high, low], axis=1)


def padded(kernel, lanes):
    return jnp.pad(kernel, ((0, 8 - V), (0, lanes - kernel.shape[1])))


def make_tables(kernel_z, kernel_x, kernel_y):
    def bf16(*shape):
        return jax.ShapeDtypeStruct(shape, jnp.bfloat16)

    return pl.pallas_call(
        tables_body,
        out_shape=(
            bf16(ROWS, 3 * EX),
            f32(V * BLK_DEV, BX, NY),
            bf16(V, 2 * DZ, 2 * EZ),
            bf16(V, EZ, 3 * DZ),
            bf16(V, 2 * NY, 2 * NY),
            bf16(V, 2 * NY, 2 * NY),
        ),
        in_specs=[VM] * 3,
        out_specs=[VM] * 6,
        compiler_params=params(32),
        name="tables",
    )(kernel_z, kernel_x, kernel_y)


def swap(even, odd, axis):
    count = lax.axis_size(axis)
    out = []
    for value, first in ((even, 0), (odd, 1)):
        pairs = []
        for i in range(first, count - 1, 2):
            pairs += [(i, i + 1), (i + 1, i)]
        out.append(lax.ppermute(value, axis, pairs))
    return out


def local(estimate0, tiles, psf_z, psf_x, psf_y, tile_pair, tile_shift):
    owners = lax.axis_size("blocks")
    all_blocks = BLK_DEV * owners
    me = lax.axis_index("blocks")
    kernel_z = padded(psf_z / jnp.sum(psf_z, axis=1, keepdims=True), 128)
    kernel_x = padded(psf_x / jnp.sum(psf_x, axis=1, keepdims=True), 128)
    kernel_y = padded(psf_y / jnp.sum(psf_y, axis=1, keepdims=True), 256)

    held = tile_pair % all_blocks // BLK_DEV
    est = estimate0
    par = jnp.stack([me % 2, lax.axis_index("depth") % 2]).astype(jnp.int32)
    *columns, cene, ceno = first_rims(par, est)
    columns = swap(*columns, "blocks")
    sent = place(held, tile_pair, tile_shift, tiles, owners)
    sent, *columns = lax.optimization_barrier((sent, *columns))
    got = lax.all_to_all(sent, "blocks", split_axis=0, concat_axis=0, tiled=True)
    tables = make_tables(kernel_z, kernel_x, kernel_y)

    count = tiles.shape[0]
    labels = got[:, BX * DZ, : 2 * count].astype(jnp.int32)
    pairs, shifts = labels[:, :count], labels[:, count:]
    mine = pairs % all_blocks // BLK_DEV == me
    live = jnp.max(mine.astype(jnp.int32), axis=1)
    got_pair = jnp.sum(jnp.where(mine, pairs, 0), axis=1)
    view = got_pair // all_blocks
    cell = jnp.where(live > 0, view * BLK_DEV + got_pair % all_blocks - me * BLK_DEV, V * BLK_DEV)
    end = lambda value: jnp.full((1,), value, jnp.int32)
    meta = jnp.concatenate([live, end(0), view, end(0), cell, end(V * BLK_DEV)])
    meta = meta.astype(jnp.int32)
    at = jnp.stack([me, lax.axis_index("depth")]).astype(jnp.int32)
    planes = lax.axis_size("depth") * DZ
    weight = weigh(planes, all_blocks, at, labels, kernel_z, kernel_x, tables[5])

    for iteration in range(ITERS):
        centre = swap(cene, ceno, "depth")
        sides = swap(*corners(par, *columns), "depth")
        pieces = (est, *columns, *centre, *sides)
        if iteration == 0:
            spread = spread_ratio(par, meta, blur_all(par, pieces, tables), got, tables)
        else:
            spread = sweep(par, meta, pieces, got, tables)
        midc, midl, midr, cene, ceno, side, sido = spread
        side, sido = swap(side, sido, "depth")
        rims = fold_rims(par, midl, midr, side, sido)
        cene, ceno, *rims = lax.optimization_barrier((cene, ceno, *rims))
        columns = swap(*rims, "blocks")
        cene, ceno = swap(cene, ceno, "depth")
        last = iteration == ITERS - 1
        est, *rest = update(par, est, weight, midc, cene, ceno, *columns, last)
        if not last:
            *columns, cene, ceno = rest
            columns = swap(*columns, "blocks")
    return est


def solution(mesh):
    in_specs = (
        P("depth", "blocks", None),
        P("blocks", "depth", None, None),
        P(),
        P(),
        P(),
        P("blocks"),
        P("blocks"),
    )
    out_specs = P("depth", "blocks", None)
    return jax.shard_map(local, mesh=mesh, in_specs=in_specs, out_specs=out_specs, check_vma=False)
```

```python
import functools

import jax
import jax.numpy as jnp
from jax import lax
from jax.experimental import pallas as pl
from jax.experimental.pallas import tpu as pltpu
from jax.sharding import PartitionSpec as P

BLK_DEV = 4
BX = 8
OFF = 8
ITERS = 2
V = 6
NY = 128
DZ = 64
DX = 32
RZ = 30
PZ = 32
RX = 16
EZ = DZ + 2 * PZ
EX = DX + 2 * RX
ROWS = V * DX
MIB = 1 << 20

exact_mode = lax.Precision.HIGHEST


def split(value):
    high = value.astype(jnp.bfloat16)
    low = (value - high.astype(jnp.float32)).astype(jnp.bfloat16)
    return high, low


def mul(a, b):
    return jnp.dot(a, b, preferred_element_type=jnp.float32)


def pair_columns(value, rows):
    return value[:, : value.shape[1] // 2], value[:, value.shape[1] // 2 :]


def blur_x(xf, planes, store):
    both = jnp.concatenate(planes, axis=1)
    high, low = split(both)
    out = mul(xf, jnp.concatenate([high, low, high], axis=0))
    store(out[:, :NY], out[:, NY:])


def starts(par, first, last):
    even = jnp.where(par[1] == 0, last, first)
    return even, first + last - even


def forward_x(par, s_ref, xf_ref, est, colse, colso, cene, ceno, side, sido):
    zeros = jnp.zeros((2,) + s_ref.shape[1:], jnp.float32)
    s_ref[0:2] = zeros
    s_ref[EZ - 2 : EZ] = zeros
    plain = par[0] == 0

    def put(base):
        def store(first, second):
            s_ref[base] = first
            s_ref[base + 1] = second

        return store

    def rim(centre, sides, start):
        @pl.loop(0, RZ // 30)
        def _(group):
            for u in range(15):
                at = 30 * group + 2 * u
                planes = []
                for z in (at, at + 1):
                    planes.append(
                        jnp.concatenate([sides[z, :RX], centre[z], sides[z, RX:]], axis=0)
                    )
                blur_x(xf_ref[...], planes, put(start + at))

    @pl.loop(0, DZ // 64)
    def _(group):
        for u in range(32):
            at = 64 * group + 2 * u
            planes = []
            for z in (at, at + 1):
                even, odd = colse[z], colso[z]
                left, right = jnp.where(plain, odd, even), jnp.where(plain, even, odd)
                planes.append(jnp.concatenate([left, est[z], right], axis=0))
            blur_x(xf_ref[...], planes, put(PZ + at))

    even, odd = starts(par, PZ - RZ, PZ + DZ)
    rim(cene, side, even)
    rim(ceno, sido, odd)


def halves(value):
    middle = value.shape[1] // 2
    return value[:, :middle], value[:, middle:]


def forward_tile(s_ref, zf_ref, yf_ref, view, row):
    field = jnp.swapaxes(s_ref[:, pl.ds(row, BX), :], 0, 1)
    parts = []
    for p in range(BX // 2):
        high, low = split(jnp.concatenate([field[2 * p], field[2 * p + 1]], axis=1))
        out = mul(zf_ref[view], jnp.concatenate([high, low], axis=0))
        parts += halves(out[:DZ] + out[DZ:])
    high, low = split(jnp.concatenate(parts, axis=0))
    first, second = halves(mul(jnp.concatenate([high, low], axis=1), yf_ref[view]))
    return first + second


def backward_tile(zb_ref, yb_ref, view, ratio):
    high, low = split(ratio)
    first, second = halves(mul(jnp.concatenate([high, low], axis=1), yb_ref[view]))
    out = first + second
    parts = []
    for p in range(BX // 2):
        at = 2 * p * DZ
        high, low = split(jnp.concatenate([out[at : at + DZ], out[at + DZ : at + 2 * DZ]], axis=1))
        parts += halves(mul(zb_ref[view], jnp.concatenate([high, low, high], axis=0)))
    return jnp.swapaxes(jnp.stack(parts, axis=0), 0, 1)


def backward_x(par, s_ref, xb_ref, midc, midl, midr, cene, ceno, side, sido):
    def spread_pair(base):
        both = jnp.concatenate([s_ref[base], s_ref[base + 1]], axis=1)
        high, low = split(both)
        out = mul(xb_ref[...], jnp.concatenate([high, low], axis=0))
        return halves(out[:EX] + out[EX:])

    def rim(centre, sides, start):
        @pl.loop(0, RZ // 30)
        def _(group):
            for u in range(15):
                at = 30 * group + 2 * u
                for i, plane in enumerate(spread_pair(start + at)):
                    sides[at + i] = jnp.concatenate([plane[:RX], plane[RX + DX :]], axis=0)
                    centre[at + i] = plane[RX : RX + DX]

    even, odd = starts(par, PZ - RZ, PZ + DZ)
    rim(cene, side, even)
    rim(ceno, sido, odd)

    @pl.loop(0, DZ // 64)
    def _(group):
        for u in range(32):
            at = 64 * group + 2 * u
            for i, plane in enumerate(spread_pair(PZ + at)):
                midl[at + i] = plane[:RX]
                midc[at + i] = plane[RX : RX + DX]
                midr[at + i] = plane[RX + DX :]


def compact(slots, meta, order):
    count = jnp.int32(0)
    for slot in range(slots):
        order[count] = slot
        count = count + meta[slot]
    order[count] = slots
    return count


def gather_x(slots, meta, order, count, fx, picked, xf, xb):
    for n in range(slots):
        slot = jnp.where(n < count, order[n], slots)
        cell = jnp.where(n < count, meta[2 * (slots + 1) + slot], 0)
        scale = jnp.where(n < count, 1.0, 0.0)
        picked[n * BX : (n + 1) * BX] = fx[cell] * scale
    table = picked[...]
    if xf is not None:
        high, low = split(table[:, :EX])
        xf[...] = jnp.concatenate([high, high, low], axis=1)
    high, low = split(table.T[:EX])
    both = jnp.concatenate([high, low], axis=0)
    xb[...] = jnp.concatenate([both, both], axis=1)


def clear_rest(slots, count, s_ref):
    @pl.loop(count, slots)
    def _(n):
        s_ref[:, pl.ds(pl.multiple_of(n * BX, BX), BX), :] = jnp.zeros((EZ, BX, NY), jnp.float32)


def fetches(slots, meta, order, moves):
    count = compact(slots, meta, order)

    @pl.loop(0, count)
    def _(k):
        slot = order[k]
        for make in moves:
            make(slot, meta[2 * (slots + 1) + slot]).start()

    def arrive(slot):
        @pl.when(slot < slots)
        def _():
            for make in moves:
                make(slot, meta[2 * (slots + 1) + slot]).wait()

    return count, arrive


def slots_of(step, k, slots, order, count):
    return [jnp.where(step * k + i < count, order[step * k + i], slots) for i in range(step)]


def blur_tiles(step, slots, meta, order, count, s_ref, zf, yf, held):
    @pl.loop(0, (count + step - 1) // step)
    def _(k):
        slot = slots_of(step, k, slots, order, count)
        out = []
        for i in range(step):
            row = pl.multiple_of((step * k + i) * BX, BX)
            out.append(forward_tile(s_ref, zf, yf, meta[slots + 1 + slot[i]], row))
        for i in range(step):
            held[slot[i]] = out[i]


def visit_tiles(step, slots, meta, order, count, arrive, s_ref, data, zb, yb, predict):
    @pl.loop(0, (count + step - 1) // step)
    def _(k):
        slot = slots_of(step, k, slots, order, count)
        for i in slot:
            arrive(i)
        view = [meta[slots + 1 + i] for i in slot]
        row = [pl.multiple_of((step * k + i) * BX, BX) for i in range(step)]
        blurred = [predict(slot[i], view[i], row[i]) for i in range(step)]
        out = [
            backward_tile(zb, yb, view[i], data[slot[i]] / blurred[i]) for i in range(step)
        ]
        for i in range(step):
            s_ref[:, pl.ds(row[i], BX), :] = out[i]


def data_move(got, data, sem):
    def make(slot, cell):
        return pltpu.make_async_copy(
            got.at[slot, pl.ds(0, BX * DZ)], data.at[slot], sem.at[slot]
        )

    return make


def sweep_body(slots, par, meta, est, colse, colso, cene, ceno, side, sido, got, fx, zf, zb, yf,
               yb, omidc, omidl, omidr, ocene, oceno, oside, osido, s_ref, order, data, sem, picked,
               xb, xf, held):
    count, arrive = fetches(slots, meta, order, [data_move(got, data, sem)])
    gather_x(slots, meta, order, count, fx, picked, xf, xb)
    forward_x(par, s_ref, xf, est, colse, colso, cene, ceno, side, sido)

    blur_tiles(4, slots, meta, order, count, s_ref, zf, yf, held)

    def predict(slot, view, row):
        return held[slot]

    visit_tiles(4, slots, meta, order, count, arrive, s_ref, data, zb, yb, predict)
    clear_rest(slots, count, s_ref)
    backward_x(par, s_ref, xb, omidc, omidl, omidr, ocene, oceno, oside, osido)


def blur_body(par, est, colse, colso, cene, ceno, side, sido, xf, zf, yf, out, s_ref, staged, sem):
    forward_x(par, s_ref, xf, est, colse, colso, cene, ceno, side, sido)

    def push(k):
        return pltpu.make_async_copy(
            staged.at[pl.ds(2 * k, 2)], out.at[pl.ds(2 * k, 2)], sem.at[k]
        )

    @pl.loop(0, V)
    def _(view):
        for i in range(BLK_DEV):
            cell = view * BLK_DEV + i
            staged[cell] = forward_tile(s_ref, zf, yf, view, pl.multiple_of(cell * BX, BX))
        push(2 * view).start()
        push(2 * view + 1).start()

    @pl.loop(0, V * BLK_DEV // 2)
    def _(k):
        push(k).wait()


def spread_body(slots, par, meta, blurred, got, far_fx, far_zb, far_yb,
                omidc, omidl, omidr, ocene, oceno, oside, osido, s_ref, order, data, sem, picked,
                xb, held, held_sem, fx, zb, yb, table_sem):
    tables = [
        pltpu.make_async_copy(far, close, table_sem.at[i])
        for i, (far, close) in enumerate(((far_fx, fx), (far_zb, zb), (far_yb, yb)))
    ]
    for copy in tables:
        copy.start()

    def make(slot, cell):
        return pltpu.make_async_copy(blurred.at[cell], held.at[slot], held_sem.at[slot])

    count, arrive = fetches(slots, meta, order, [make, data_move(got, data, sem)])
    for copy in tables:
        copy.wait()
    gather_x(slots, meta, order, count, fx, picked, None, xb)

    def predict(slot, view, row):
        return held[slot]

    visit_tiles(4, slots, meta, order, count, arrive, s_ref, data, zb, yb, predict)
    clear_rest(slots, count, s_ref)
    backward_x(par, s_ref, xb, omidc, omidl, omidr, ocene, oceno, oside, osido)


def f32(*shape):
    return jax.ShapeDtypeStruct(shape, jnp.float32)


VM = pl.BlockSpec(memory_space=pltpu.VMEM)
SM = pl.BlockSpec(memory_space=pltpu.SMEM)
PIECES = (
    f32(DZ, DX, NY),
    f32(DZ, RX, NY),
    f32(DZ, RX, NY),
    f32(RZ, DX, NY),
    f32(RZ, DX, NY),
    f32(RZ, 2 * RX, NY),
    f32(RZ, 2 * RX, NY),
)


def params(mib):
    return pltpu.CompilerParams(vmem_limit_bytes=mib * MIB)


def visit_scratch(slots):
    rows = slots * BX
    return [
        pltpu.VMEM((EZ, rows, NY), jnp.float32),
        pltpu.SMEM((slots + 1,), jnp.int32),
        pltpu.VMEM((slots + 1, BX * DZ, NY), jnp.float32),
        pltpu.SemaphoreType.DMA((slots + 1,)),
        pltpu.VMEM((rows, NY), jnp.float32),
        pltpu.VMEM((2 * EX, 2 * rows), jnp.bfloat16),
    ]


HB = pl.BlockSpec(memory_space=pltpu.HBM)


def in_hbm(value):
    return pltpu.with_memory_space_constraint(value, pltpu.HBM)


def sweep(par, meta, pieces, got, tables):
    slots = got.shape[0]
    return pl.pallas_call(
        functools.partial(sweep_body, slots),
        out_shape=PIECES,
        in_specs=[SM] * 2 + [VM] * 7 + [HB] + [VM] * 5,
        out_specs=[VM] * 7,
        scratch_shapes=visit_scratch(slots)
        + [
            pltpu.VMEM((slots * BX, 3 * EX), jnp.bfloat16),
            pltpu.VMEM((slots + 1, BX * DZ, NY), jnp.float32),
        ],
        compiler_params=params(36),
        name="sweep",
    )(par, meta, *pieces, in_hbm(got), *tables[1:])


def blur_all(par, pieces, tables):
    xf, fx, zf, zb, yf, yb = tables
    cells = V * BLK_DEV
    return pl.pallas_call(
        blur_body,
        out_shape=pltpu.HBM((cells, BX * DZ, NY), jnp.float32),
        in_specs=[SM] + [VM] * 10,
        out_specs=HB,
        scratch_shapes=[
            pltpu.VMEM((EZ, ROWS, NY), jnp.float32),
            pltpu.VMEM((cells, BX * DZ, NY), jnp.float32),
            pltpu.SemaphoreType.DMA((cells // 2,)),
        ],
        compiler_params=params(34),
        name="blur_all",
    )(par, *pieces, xf, zf, yf)


def spread_ratio(par, meta, blurred, got, tables):
    slots = got.shape[0]
    xf, fx, zf, zb, yf, yb = tables
    return pl.pallas_call(
        functools.partial(spread_body, slots),
        out_shape=PIECES,
        in_specs=[SM] * 2 + [HB] * 5,
        out_specs=[VM] * 7,
        scratch_shapes=visit_scratch(slots)
        + [
            pltpu.VMEM((slots + 1, BX * DZ, NY), jnp.float32),
            pltpu.SemaphoreType.DMA((slots + 1,)),
        ]
        + [pltpu.VMEM(table.shape, table.dtype) for table in (fx, zb, yb)]
        + [pltpu.SemaphoreType.DMA((3,))],
        compiler_params=params(36),
        name="spread_ratio",
    )(par, meta, *[in_hbm(value) for value in (blurred, got, fx, zb, yb)])


def place_body(owner, pair, shift, tiles, out, staged, labels, sem, label_sem):
    count = tiles.shape[0]
    slots = out.shape[0]
    lane = lax.broadcasted_iota(jnp.int32, (8, NY), 1)
    values = jnp.zeros((8, NY), jnp.int32)
    for k in range(count):
        values = jnp.where(lane == k, pair[k], values)
        values = jnp.where(lane == count + k, shift[k], values)
    labels[...] = values.astype(jnp.float32)
    copies = []
    for slot in range(slots):
        copies.append(
            pltpu.make_async_copy(
                labels, out.at[slot, pl.ds(BX * DZ, 8)], label_sem.at[slot]
            )
        )
        copies[-1].start()
    column = lax.broadcasted_iota(jnp.int32, (DZ, BX, NY), 2)
    for k in range(count):
        moved = pltpu.roll(tiles[k], (shift[k] + NY) % NY, 2)
        source = column - shift[k]
        moved = jnp.where((source >= 0) & (source < NY), moved, 0.0)
        staged[k] = jnp.swapaxes(moved, 0, 1).reshape(BX * DZ, NY)
        copies.append(
            pltpu.make_async_copy(staged.at[k], out.at[owner[k], pl.ds(0, BX * DZ)], sem.at[k])
        )
        copies[-1].start()
    for copy in copies:
        copy.wait()


def place(owner, pair, shift, tiles, slots):
    count = tiles.shape[0]
    return pl.pallas_call(
        place_body,
        out_shape=pltpu.HBM((slots, BX * DZ + 8, NY), jnp.float32),
        in_specs=[SM, SM, SM, VM],
        out_specs=HB,
        scratch_shapes=[
            pltpu.VMEM((count, BX * DZ, NY), jnp.float32),
            pltpu.VMEM((8, NY), jnp.float32),
            pltpu.SemaphoreType.DMA((count,)),
            pltpu.SemaphoreType.DMA((slots,)),
        ],
        compiler_params=params(32),
        name="place",
    )(owner, pair, shift, tiles)


def pick(par, even_if_plain, other):
    plain = par[0] == 0
    return jnp.where(plain, even_if_plain, other), jnp.where(plain, other, even_if_plain)


def first_body(par, est, colse, colso, cene, ceno):
    @pl.loop(0, DZ // 4)
    def _(group):
        for u in range(4):
            z = 4 * group + u
            colse[z], colso[z] = pick(par, est[z, RX:], est[z, :RX])

    even, odd = starts(par, 0, DZ - RZ)

    @pl.loop(0, RZ // 6)
    def _(group):
        for u in range(6):
            k = 6 * group + u
            cene[k] = est[even + k]
            ceno[k] = est[odd + k]


COLUMNS = f32(DZ, RX, NY)
PLANES = f32(RZ, DX, NY)


def first_rims(par, est):
    return pl.pallas_call(
        first_body,
        out_shape=(COLUMNS, COLUMNS, PLANES, PLANES),
        in_specs=[SM, VM],
        out_specs=[VM] * 4,
        compiler_params=params(16),
        name="first_rims",
    )(par, est)


def rims_body(par, midl, midr, side, sido, outl, outr):
    even, odd = starts(par, 0, DZ - RZ)

    @pl.loop(0, DZ // 4)
    def _(group):
        for u in range(4):
            z = 4 * group + u
            outl[z], outr[z] = pick(par, midr[z], midl[z])

    for start, sides in ((even, side), (odd, sido)):

        @pl.loop(0, RZ // 6)
        def _(group):
            for u in range(6):
                k = 6 * group + u
                add, other = pick(par, sides[k, RX:], sides[k, :RX])
                outl[start + k] += add
                outr[start + k] += other


def fold_rims(par, midl, midr, side, sido):
    return pl.pallas_call(
        rims_body,
        out_shape=(COLUMNS, COLUMNS),
        in_specs=[SM] + [VM] * 4,
        out_specs=[VM] * 2,
        compiler_params=params(16),
        name="fold_rims",
    )(par, midl, midr, side, sido)


def corner_body(par, colse, colso, side, sido):
    even, odd = starts(par, 0, DZ - RZ)
    for start, out in ((even, side), (odd, sido)):

        @pl.loop(0, RZ // 6)
        def _(group):
            for u in range(6):
                k = 6 * group + u
                right, left = pick(par, colse[start + k], colso[start + k])
                out[k] = jnp.concatenate([left, right], axis=0)


def corners(par, colse, colso):
    return pl.pallas_call(
        corner_body,
        out_shape=(PLANES, PLANES),
        in_specs=[SM] + [VM] * 2,
        out_specs=[VM] * 2,
        compiler_params=params(16),
        name="corners",
    )(par, colse, colso)


def weigh_body(planes, blocks, at, labels, kz, kx, yb, out, along_x, inside, views):
    held = labels.shape[1] // 2
    lane = lax.broadcasted_iota(jnp.int32, (1, NY), 1)
    boxes = kx[...]
    for i in range(1, BX):
        boxes = boxes + pltpu.roll(kx[...], i, 1)
    along_x[...] = jnp.zeros(along_x.shape, jnp.float32)
    inside[...] = jnp.zeros(inside.shape, jnp.float32)
    views[...] = jnp.full(views.shape, -1, jnp.int32)

    @pl.loop(0, labels.shape[0])
    def _(holder):
        for k in range(held):
            pair = labels[holder, k]
            shift = labels[holder, held + k]
            view = pair // blocks
            beside = pair % blocks - at[0] * BLK_DEV

            @pl.when((beside >= -2) & (beside < BLK_DEV + 2))
            def _():
                row = holder * held + k
                box = jnp.zeros((1, NY), jnp.float32)
                for v in range(V):
                    box = jnp.where(view == v, boxes[v : v + 1], box)
                step = (BX * beside - 15 + NY) % NY
                moved = pltpu.roll(jnp.broadcast_to(box, (8, NY)), step, 1)
                along_x[pl.ds(row, 1), :] = moved[:1]
                seen = (lane >= shift) & (lane < NY + shift)
                inside[pl.ds(row, 1), :] = jnp.where(seen, 1.0, 0.0)
                views[pl.ds(row, 1), :] = jnp.full((1, NY), view, jnp.int32)

    z = at[1] * DZ + lax.broadcasted_iota(jnp.int32, (DZ, NY), 0)
    tap = lax.broadcasted_iota(jnp.int32, (DZ, NY), 1)
    reached = (z - tap + RZ >= 0) & (z - tap + RZ < planes)
    seen = inside[...].astype(jnp.bfloat16)
    gains, slopes = [], []
    for v in range(V):
        first, second = halves(mul(seen, yb[v, :NY]))
        member = jnp.where(views[...] == v, along_x[...], 0.0)
        gains.append(
            lax.dot_general(
                member.T[:DX],
                first + second,
                (((1,), (0,)), ((), ())),
                precision=exact_mode,
                preferred_element_type=jnp.float32,
            )
        )
        row = jnp.where(reached, jnp.broadcast_to(kz[v : v + 1], (DZ, NY)), 0.0)
        slopes.append(jnp.broadcast_to(jnp.sum(row, axis=1, keepdims=True), (DZ, NY)))
    for i in range(DZ):
        total = slopes[0][i : i + 1] * gains[0]
        for v in range(1, V):
            total = total + slopes[v][i : i + 1] * gains[v]
        out[i] = jnp.maximum(total, 1.0)


def weigh(planes, blocks, at, labels, kz, kx, yb):
    count = labels.shape[0] * labels.shape[1] // 2
    return pl.pallas_call(
        functools.partial(weigh_body, planes, blocks),
        out_shape=f32(DZ, DX, NY),
        in_specs=[SM] * 2 + [VM] * 3,
        out_specs=VM,
        scratch_shapes=[
            pltpu.VMEM((count, NY), jnp.float32),
            pltpu.VMEM((count, NY), jnp.float32),
            pltpu.VMEM((count, NY), jnp.int32),
        ],
        compiler_params=params(16),
        name="weigh",
    )(at, labels, kz, kx, yb)


def update_body(par, est, weight, midc, cene, ceno, colse, colso, new, *outs):
    even, odd = starts(par, 0, DZ - RZ)

    @pl.loop(0, DZ // 4)
    def _(group):
        for u in range(4):
            z = 4 * group + u
            right, left = pick(par, colse[z], colso[z])
            new[z] = midc[z] + jnp.concatenate([left, right], axis=0)

    for start, centre in ((even, cene), (odd, ceno)):

        @pl.loop(0, RZ // 6)
        def _(group):
            for u in range(6):
                new[start + 6 * group + u] += centre[6 * group + u]

    @pl.loop(0, DZ // 4)
    def _(group):
        for u in range(4):
            z = 4 * group + u
            value = est[z] * new[z] / weight[z]
            new[z] = value
            if outs:
                outs[0][z], outs[1][z] = pick(par, value[RX:], value[:RX])

    if outs:

        @pl.loop(0, RZ // 6)
        def _(group):
            for u in range(6):
                k = 6 * group + u
                outs[2][k] = new[even + k]
                outs[3][k] = new[odd + k]


def update(par, est, weight, midc, cene, ceno, colse, colso, last):
    shapes = [f32(DZ, DX, NY)]
    if not last:
        shapes += [COLUMNS, COLUMNS, PLANES, PLANES]
    return pl.pallas_call(
        update_body,
        out_shape=tuple(shapes),
        in_specs=[SM] + [VM] * 7,
        out_specs=[VM] * len(shapes),
        compiler_params=params(16),
        name="update",
    )(par, est, weight, midc, cene, ceno, colse, colso)


def band(row, rows, first):
    table = jnp.broadcast_to(row, (rows, row.shape[1]))
    return pltpu.roll(table, first % row.shape[1], 1, stride=1, stride_axis=0)


def tables_body(kz, kx, ky, xf, fx, zf, zb, yf, yb):
    for view in range(V):
        full = band(kz[view : view + 1], DZ, PZ - RZ)
        high, low = split(full)
        zf[view] = jnp.concatenate(
            [jnp.concatenate([high, high], axis=1), jnp.concatenate([low, low], axis=1)], axis=0
        )
        high, low = split(full.T)
        zb[view] = jnp.concatenate([high, high, low], axis=1)
        full = band(ky[view : view + 1], NY, -15)[:, :NY]
        high, low = split(full)
        half = jnp.concatenate([high, low], axis=1)
        yb[view] = jnp.concatenate([half, half], axis=0)
        high, low = split(full.T)
        half = jnp.concatenate([high, low], axis=1)
        yf[view] = jnp.concatenate([half, half], axis=0)
    full = jnp.concatenate([band(kx[v : v + 1], DX, RX - 15) for v in range(V)], axis=0)
    fx[...] = full.reshape(V * BLK_DEV, BX, NY)
    high, low = split(full[:, :EX])
    xf[...] = jnp.concatenate([high, high, low], axis=1)


def padded(kernel, lanes):
    return jnp.pad(kernel, ((0, 8 - V), (0, lanes - kernel.shape[1])))


def make_tables(kernel_z, kernel_x, kernel_y):
    def bf16(*shape):
        return jax.ShapeDtypeStruct(shape, jnp.bfloat16)

    return pl.pallas_call(
        tables_body,
        out_shape=(
            bf16(ROWS, 3 * EX),
            f32(V * BLK_DEV, BX, NY),
            bf16(V, 2 * DZ, 2 * EZ),
            bf16(V, EZ, 3 * DZ),
            bf16(V, 2 * NY, 2 * NY),
            bf16(V, 2 * NY, 2 * NY),
        ),
        in_specs=[VM] * 3,
        out_specs=[VM] * 6,
        compiler_params=params(32),
        name="tables",
    )(kernel_z, kernel_x, kernel_y)


def swap(even, odd, axis):
    count = lax.axis_size(axis)
    out = []
    for value, first in ((odd, 1), (even, 0)):
        pairs = []
        for i in range(first, count - 1, 2):
            pairs += [(i, i + 1), (i + 1, i)]
        out.append(lax.ppermute(value, axis, pairs))
    return out[::-1]


def local(estimate0, tiles, psf_z, psf_x, psf_y, tile_pair, tile_shift):
    owners = lax.axis_size("blocks")
    all_blocks = BLK_DEV * owners
    me = lax.axis_index("blocks")
    kernel_z = padded(psf_z / jnp.sum(psf_z, axis=1, keepdims=True), 128)
    kernel_x = padded(psf_x / jnp.sum(psf_x, axis=1, keepdims=True), 128)
    kernel_y = padded(psf_y / jnp.sum(psf_y, axis=1, keepdims=True), 256)

    held = tile_pair % all_blocks // BLK_DEV
    est = estimate0
    par = jnp.stack([me % 2, lax.axis_index("depth") % 2]).astype(jnp.int32)
    *columns, cene, ceno = first_rims(par, est)
    columns = swap(*columns, "blocks")
    sent = place(held, tile_pair, tile_shift, tiles, owners)
    sent, *columns = lax.optimization_barrier((sent, *columns))
    got = lax.all_to_all(sent, "blocks", split_axis=0, concat_axis=0, tiled=True)
    tables = make_tables(kernel_z, kernel_x, kernel_y)

    count = tiles.shape[0]
    labels = got[:, BX * DZ, : 2 * count].astype(jnp.int32)
    pairs, shifts = labels[:, :count], labels[:, count:]
    mine = pairs % all_blocks // BLK_DEV == me
    live = jnp.max(mine.astype(jnp.int32), axis=1)
    got_pair = jnp.sum(jnp.where(mine, pairs, 0), axis=1)
    view = got_pair // all_blocks
    cell = jnp.where(live > 0, view * BLK_DEV + got_pair % all_blocks - me * BLK_DEV, V * BLK_DEV)
    end = lambda value: jnp.full((1,), value, jnp.int32)
    meta = jnp.concatenate([live, end(0), view, end(0), cell, end(V * BLK_DEV)])
    meta = meta.astype(jnp.int32)
    at = jnp.stack([me, lax.axis_index("depth")]).astype(jnp.int32)
    planes = lax.axis_size("depth") * DZ
    weight = weigh(planes, all_blocks, at, labels, kernel_z, kernel_x, tables[5])

    for iteration in range(ITERS):
        centre = swap(cene, ceno, "depth")
        sides = swap(*corners(par, *columns), "depth")
        pieces = (est, *columns, *centre, *sides)
        if iteration == 0:
            spread = spread_ratio(par, meta, blur_all(par, pieces, tables), got, tables)
        else:
            spread = sweep(par, meta, pieces, got, tables)
        midc, midl, midr, cene, ceno, side, sido = spread
        side, sido = swap(side, sido, "depth")
        rims = fold_rims(par, midl, midr, side, sido)
        cene, ceno, *rims = lax.optimization_barrier((cene, ceno, *rims))
        columns = swap(*rims, "blocks")
        cene, ceno = swap(cene, ceno, "depth")
        last = iteration == ITERS - 1
        est, *rest = update(par, est, weight, midc, cene, ceno, *columns, last)
        if not last:
            *columns, cene, ceno = rest
            columns = swap(*columns, "blocks")
    return est


def solution(mesh):
    in_specs = (
        P("depth", "blocks", None),
        P("blocks", "depth", None, None),
        P(),
        P(),
        P(),
        P("blocks"),
        P("blocks"),
    )
    out_specs = P("depth", "blocks", None)
    return jax.shard_map(local, mesh=mesh, in_specs=in_specs, out_specs=out_specs, check_vma=False)
```

```python
import functools

import jax
import jax.numpy as jnp
from jax import lax
from jax.experimental import pallas as pl
from jax.experimental.pallas import tpu as pltpu
from jax.sharding import PartitionSpec as P

BLK_DEV = 4
BX = 8
OFF = 8
ITERS = 2
V = 6
NY = 128
DZ = 64
DX = 32
RZ = 30
PZ = 32
RX = 16
EZ = DZ + 2 * PZ
EX = DX + 2 * RX
ROWS = V * DX
MIB = 1 << 20

exact_mode = lax.Precision.HIGHEST


def split(value):
    high = value.astype(jnp.bfloat16)
    low = (value - high.astype(jnp.float32)).astype(jnp.bfloat16)
    return high, low


def mul(a, b):
    return jnp.dot(a, b, preferred_element_type=jnp.float32)


def pair_columns(value, rows):
    return value[:, : value.shape[1] // 2], value[:, value.shape[1] // 2 :]


def blur_x(xf, planes, store):
    both = jnp.concatenate(planes, axis=1)
    high, low = split(both)
    out = mul(xf, jnp.concatenate([high, low, high], axis=0))
    store(out[:, :NY], out[:, NY:])


def starts(par, first, last):
    even = jnp.where(par[1] == 0, last, first)
    return even, first + last - even


def forward_x(par, s_ref, xf_ref, est, colse, colso, cene, ceno, side, sido):
    zeros = jnp.zeros((2,) + s_ref.shape[1:], jnp.float32)
    s_ref[0:2] = zeros
    s_ref[EZ - 2 : EZ] = zeros
    plain = par[0] == 0

    def put(base):
        def store(first, second):
            s_ref[base] = first
            s_ref[base + 1] = second

        return store

    def rim(centre, sides, start):
        @pl.loop(0, RZ // 30)
        def _(group):
            for u in range(15):
                at = 30 * group + 2 * u
                planes = []
                for z in (at, at + 1):
                    planes.append(
                        jnp.concatenate([sides[z, :RX], centre[z], sides[z, RX:]], axis=0)
                    )
                blur_x(xf_ref[...], planes, put(start + at))

    @pl.loop(0, DZ // 64)
    def _(group):
        for u in range(32):
            at = 64 * group + 2 * u
            planes = []
            for z in (at, at + 1):
                even, odd = colse[z], colso[z]
                left, right = jnp.where(plain, odd, even), jnp.where(plain, even, odd)
                planes.append(jnp.concatenate([left, est[z], right], axis=0))
            blur_x(xf_ref[...], planes, put(PZ + at))

    even, odd = starts(par, PZ - RZ, PZ + DZ)
    rim(cene, side, even)
    rim(ceno, sido, odd)


def halves(value):
    middle = value.shape[1] // 2
    return value[:, :middle], value[:, middle:]


def forward_tile(s_ref, zf_ref, yf_ref, view, row):
    field = jnp.swapaxes(s_ref[:, pl.ds(row, BX), :], 0, 1)
    parts = []
    for p in range(BX // 2):
        high, low = split(jnp.concatenate([field[2 * p], field[2 * p + 1]], axis=1))
        out = mul(zf_ref[view], jnp.concatenate([high, low], axis=0))
        parts += halves(out[:DZ] + out[DZ:])
    high, low = split(jnp.concatenate(parts, axis=0))
    first, second = halves(mul(jnp.concatenate([high, low], axis=1), yf_ref[view]))
    return first + second


def backward_tile(zb_ref, yb_ref, view, ratio):
    high, low = split(ratio)
    first, second = halves(mul(jnp.concatenate([high, low], axis=1), yb_ref[view]))
    out = first + second
    parts = []
    for p in range(BX // 2):
        at = 2 * p * DZ
        high, low = split(jnp.concatenate([out[at : at + DZ], out[at + DZ : at + 2 * DZ]], axis=1))
        parts += halves(mul(zb_ref[view], jnp.concatenate([high, low, high], axis=0)))
    return jnp.swapaxes(jnp.stack(parts, axis=0), 0, 1)


def backward_x(par, s_ref, xb_ref, midc, midl, midr, cene, ceno, side, sido):
    def spread_pair(base):
        both = jnp.concatenate([s_ref[base], s_ref[base + 1]], axis=1)
        high, low = split(both)
        out = mul(xb_ref[...], jnp.concatenate([high, low], axis=0))
        return halves(out[:EX] + out[EX:])

    def rim(centre, sides, start):
        @pl.loop(0, RZ // 30)
        def _(group):
            for u in range(15):
                at = 30 * group + 2 * u
                for i, plane in enumerate(spread_pair(start + at)):
                    sides[at + i] = jnp.concatenate([plane[:RX], plane[RX + DX :]], axis=0)
                    centre[at + i] = plane[RX : RX + DX]

    even, odd = starts(par, PZ - RZ, PZ + DZ)
    rim(cene, side, even)
    rim(ceno, sido, odd)

    @pl.loop(0, DZ // 64)
    def _(group):
        for u in range(32):
            at = 64 * group + 2 * u
            for i, plane in enumerate(spread_pair(PZ + at)):
                midl[at + i] = plane[:RX]
                midc[at + i] = plane[RX : RX + DX]
                midr[at + i] = plane[RX + DX :]


def compact(slots, meta, order):
    count = jnp.int32(0)
    for slot in range(slots):
        order[count] = slot
        count = count + meta[slot]
    order[count] = slots
    return count


def gather_x(slots, meta, order, count, fx, picked, xf, xb):
    for n in range(slots):
        slot = jnp.where(n < count, order[n], slots)
        cell = jnp.where(n < count, meta[2 * (slots + 1) + slot], 0)
        scale = jnp.where(n < count, 1.0, 0.0)
        picked[n * BX : (n + 1) * BX] = fx[cell] * scale
    table = picked[...]
    if xf is not None:
        high, low = split(table[:, :EX])
        xf[...] = jnp.concatenate([high, high, low], axis=1)
    high, low = split(table.T[:EX])
    both = jnp.concatenate([high, low], axis=0)
    xb[...] = jnp.concatenate([both, both], axis=1)


def clear_rest(slots, count, s_ref):
    @pl.loop(count, slots)
    def _(n):
        s_ref[:, pl.ds(pl.multiple_of(n * BX, BX), BX), :] = jnp.zeros((EZ, BX, NY), jnp.float32)


def fetches(slots, meta, order, moves):
    count = compact(slots, meta, order)

    @pl.loop(0, count)
    def _(k):
        slot = order[k]
        for make in moves:
            make(slot, meta[2 * (slots + 1) + slot]).start()

    def arrive(slot):
        @pl.when(slot < slots)
        def _():
            for make in moves:
                make(slot, meta[2 * (slots + 1) + slot]).wait()

    return count, arrive


def slots_of(step, k, slots, order, count):
    return [jnp.where(step * k + i < count, order[step * k + i], slots) for i in range(step)]


def blur_tiles(step, slots, meta, order, count, s_ref, zf, yf, held):
    @pl.loop(0, (count + step - 1) // step)
    def _(k):
        slot = slots_of(step, k, slots, order, count)
        out = []
        for i in range(step):
            row = pl.multiple_of((step * k + i) * BX, BX)
            out.append(forward_tile(s_ref, zf, yf, meta[slots + 1 + slot[i]], row))
        for i in range(step):
            held[slot[i]] = out[i]


def visit_tiles(step, slots, meta, order, count, arrive, s_ref, data, zb, yb, predict):
    @pl.loop(0, (count + step - 1) // step)
    def _(k):
        slot = slots_of(step, k, slots, order, count)
        for i in slot:
            arrive(i)
        view = [meta[slots + 1 + i] for i in slot]
        row = [pl.multiple_of((step * k + i) * BX, BX) for i in range(step)]
        blurred = [predict(slot[i], view[i], row[i]) for i in range(step)]
        out = [
            backward_tile(zb, yb, view[i], data[slot[i]] / blurred[i]) for i in range(step)
        ]
        for i in range(step):
            s_ref[:, pl.ds(row[i], BX), :] = out[i]


def data_move(got, data, sem):
    def make(slot, cell):
        return pltpu.make_async_copy(
            got.at[slot, pl.ds(0, BX * DZ)], data.at[slot], sem.at[slot]
        )

    return make


def sweep_body(slots, par, meta, est, colse, colso, cene, ceno, side, sido, got, fx, zf, zb, yf,
               yb, omidc, omidl, omidr, ocene, oceno, oside, osido, s_ref, order, data, sem, picked,
               xb, xf, held):
    count, arrive = fetches(slots, meta, order, [data_move(got, data, sem)])
    gather_x(slots, meta, order, count, fx, picked, xf, xb)
    forward_x(par, s_ref, xf, est, colse, colso, cene, ceno, side, sido)

    blur_tiles(4, slots, meta, order, count, s_ref, zf, yf, held)

    def predict(slot, view, row):
        return held[slot]

    visit_tiles(4, slots, meta, order, count, arrive, s_ref, data, zb, yb, predict)
    clear_rest(slots, count, s_ref)
    backward_x(par, s_ref, xb, omidc, omidl, omidr, ocene, oceno, oside, osido)


def blur_body(par, est, colse, colso, cene, ceno, side, sido, xf, zf, yf, out, s_ref, staged, sem):
    forward_x(par, s_ref, xf, est, colse, colso, cene, ceno, side, sido)

    def push(k):
        return pltpu.make_async_copy(
            staged.at[pl.ds(2 * k, 2)], out.at[pl.ds(2 * k, 2)], sem.at[k]
        )

    @pl.loop(0, V)
    def _(view):
        for i in range(BLK_DEV):
            cell = view * BLK_DEV + i
            staged[cell] = forward_tile(s_ref, zf, yf, view, pl.multiple_of(cell * BX, BX))
        push(2 * view).start()
        push(2 * view + 1).start()

    @pl.loop(0, V * BLK_DEV // 2)
    def _(k):
        push(k).wait()


def spread_body(slots, par, meta, blurred, got, far_fx, far_zb, far_yb,
                omidc, omidl, omidr, ocene, oceno, oside, osido, s_ref, order, data, sem, picked,
                xb, held, held_sem, fx, zb, yb, table_sem):
    tables = [
        pltpu.make_async_copy(far, close, table_sem.at[i])
        for i, (far, close) in enumerate(((far_fx, fx), (far_zb, zb), (far_yb, yb)))
    ]
    for copy in tables:
        copy.start()

    def make(slot, cell):
        return pltpu.make_async_copy(blurred.at[cell], held.at[slot], held_sem.at[slot])

    count, arrive = fetches(slots, meta, order, [make, data_move(got, data, sem)])
    for copy in tables:
        copy.wait()
    gather_x(slots, meta, order, count, fx, picked, None, xb)

    def predict(slot, view, row):
        return held[slot]

    visit_tiles(4, slots, meta, order, count, arrive, s_ref, data, zb, yb, predict)
    clear_rest(slots, count, s_ref)
    backward_x(par, s_ref, xb, omidc, omidl, omidr, ocene, oceno, oside, osido)


def f32(*shape):
    return jax.ShapeDtypeStruct(shape, jnp.float32)


VM = pl.BlockSpec(memory_space=pltpu.VMEM)
SM = pl.BlockSpec(memory_space=pltpu.SMEM)
PIECES = (
    f32(DZ, DX, NY),
    f32(DZ, RX, NY),
    f32(DZ, RX, NY),
    f32(RZ, DX, NY),
    f32(RZ, DX, NY),
    f32(RZ, 2 * RX, NY),
    f32(RZ, 2 * RX, NY),
)


def params(mib):
    return pltpu.CompilerParams(vmem_limit_bytes=mib * MIB)


def visit_scratch(slots):
    rows = slots * BX
    return [
        pltpu.VMEM((EZ, rows, NY), jnp.float32),
        pltpu.SMEM((slots + 1,), jnp.int32),
        pltpu.VMEM((slots + 1, BX * DZ, NY), jnp.float32),
        pltpu.SemaphoreType.DMA((slots + 1,)),
        pltpu.VMEM((rows, NY), jnp.float32),
        pltpu.VMEM((2 * EX, 2 * rows), jnp.bfloat16),
    ]


HB = pl.BlockSpec(memory_space=pltpu.HBM)


def in_hbm(value):
    return pltpu.with_memory_space_constraint(value, pltpu.HBM)


def sweep(par, meta, pieces, got, tables):
    slots = got.shape[0]
    return pl.pallas_call(
        functools.partial(sweep_body, slots),
        out_shape=PIECES,
        in_specs=[SM] * 2 + [VM] * 7 + [HB] + [VM] * 5,
        out_specs=[VM] * 7,
        scratch_shapes=visit_scratch(slots)
        + [
            pltpu.VMEM((slots * BX, 3 * EX), jnp.bfloat16),
            pltpu.VMEM((slots + 1, BX * DZ, NY), jnp.float32),
        ],
        compiler_params=params(36),
        name="sweep",
    )(par, meta, *pieces, in_hbm(got), *tables[1:])


def blur_all(par, pieces, tables):
    xf, fx, zf, zb, yf, yb = tables
    cells = V * BLK_DEV
    return pl.pallas_call(
        blur_body,
        out_shape=pltpu.HBM((cells, BX * DZ, NY), jnp.float32),
        in_specs=[SM] + [VM] * 10,
        out_specs=HB,
        scratch_shapes=[
            pltpu.VMEM((EZ, ROWS, NY), jnp.float32),
            pltpu.VMEM((cells, BX * DZ, NY), jnp.float32),
            pltpu.SemaphoreType.DMA((cells // 2,)),
        ],
        compiler_params=params(34),
        name="blur_all",
    )(par, *pieces, xf, zf, yf)


def spread_ratio(par, meta, blurred, got, tables):
    slots = got.shape[0]
    xf, fx, zf, zb, yf, yb = tables
    return pl.pallas_call(
        functools.partial(spread_body, slots),
        out_shape=PIECES,
        in_specs=[SM] * 2 + [HB] * 5,
        out_specs=[VM] * 7,
        scratch_shapes=visit_scratch(slots)
        + [
            pltpu.VMEM((slots + 1, BX * DZ, NY), jnp.float32),
            pltpu.SemaphoreType.DMA((slots + 1,)),
        ]
        + [pltpu.VMEM(table.shape, table.dtype) for table in (fx, zb, yb)]
        + [pltpu.SemaphoreType.DMA((3,))],
        compiler_params=params(36),
        name="spread_ratio",
    )(par, meta, *[in_hbm(value) for value in (blurred, got, fx, zb, yb)])


def place_body(owner, pair, shift, tiles, out, staged, labels, sem, label_sem):
    count = tiles.shape[0]
    slots = out.shape[0]
    lane = lax.broadcasted_iota(jnp.int32, (8, NY), 1)
    values = jnp.zeros((8, NY), jnp.int32)
    for k in range(count):
        values = jnp.where(lane == k, pair[k], values)
        values = jnp.where(lane == count + k, shift[k], values)
    labels[...] = values.astype(jnp.float32)
    copies = []
    for slot in range(slots):
        copies.append(
            pltpu.make_async_copy(
                labels, out.at[slot, pl.ds(BX * DZ, 8)], label_sem.at[slot]
            )
        )
        copies[-1].start()
    column = lax.broadcasted_iota(jnp.int32, (DZ, BX, NY), 2)
    for k in range(count):
        moved = pltpu.roll(tiles[k], (shift[k] + NY) % NY, 2)
        source = column - shift[k]
        moved = jnp.where((source >= 0) & (source < NY), moved, 0.0)
        staged[k] = jnp.swapaxes(moved, 0, 1).reshape(BX * DZ, NY)
        copies.append(
            pltpu.make_async_copy(staged.at[k], out.at[owner[k], pl.ds(0, BX * DZ)], sem.at[k])
        )
        copies[-1].start()
    for copy in copies:
        copy.wait()


def place(owner, pair, shift, tiles, slots):
    count = tiles.shape[0]
    return pl.pallas_call(
        place_body,
        out_shape=pltpu.HBM((slots, BX * DZ + 8, NY), jnp.float32),
        in_specs=[SM, SM, SM, VM],
        out_specs=HB,
        scratch_shapes=[
            pltpu.VMEM((count, BX * DZ, NY), jnp.float32),
            pltpu.VMEM((8, NY), jnp.float32),
            pltpu.SemaphoreType.DMA((count,)),
            pltpu.SemaphoreType.DMA((slots,)),
        ],
        compiler_params=params(32),
        name="place",
    )(owner, pair, shift, tiles)


def pick(par, even_if_plain, other):
    plain = par[0] == 0
    return jnp.where(plain, even_if_plain, other), jnp.where(plain, other, even_if_plain)


def pull(pairs, sem):
    copies = [
        pltpu.make_async_copy(source, target, sem.at[i])
        for i, (source, target) in enumerate(pairs)
    ]
    for copy in copies:
        copy.start()
    for copy in copies:
        copy.wait()


def columns_body(par, est, colse, colso, sem):
    even = pl.multiple_of(jnp.where(par[0] == 0, RX, 0), RX)
    odd = pl.multiple_of(RX - even, RX)
    pull([(est.at[:, pl.ds(even, RX)], colse), (est.at[:, pl.ds(odd, RX)], colso)], sem)


def planes_body(par, est, cene, ceno, sem):
    even, odd = starts(par, 0, DZ - RZ)
    pull([(est.at[pl.ds(even, RZ)], cene), (est.at[pl.ds(odd, RZ)], ceno)], sem)


COLUMNS = f32(DZ, RX, NY)
PLANES = f32(RZ, DX, NY)


def first(body, name, shape, par, est):
    return pl.pallas_call(
        body,
        out_shape=(shape, shape),
        in_specs=[SM, HB],
        out_specs=[VM] * 2,
        scratch_shapes=[pltpu.SemaphoreType.DMA((2,))],
        compiler_params=params(16),
        name=name,
    )(par, in_hbm(est))


def rims_body(par, midl, midr, side, sido, outl, outr):
    even, odd = starts(par, 0, DZ - RZ)

    @pl.loop(0, DZ // 4)
    def _(group):
        for u in range(4):
            z = 4 * group + u
            outl[z], outr[z] = pick(par, midr[z], midl[z])

    for start, sides in ((even, side), (odd, sido)):

        @pl.loop(0, RZ // 6)
        def _(group):
            for u in range(6):
                k = 6 * group + u
                add, other = pick(par, sides[k, RX:], sides[k, :RX])
                outl[start + k] += add
                outr[start + k] += other


def fold_rims(par, midl, midr, side, sido):
    return pl.pallas_call(
        rims_body,
        out_shape=(COLUMNS, COLUMNS),
        in_specs=[SM] + [VM] * 4,
        out_specs=[VM] * 2,
        compiler_params=params(16),
        name="fold_rims",
    )(par, midl, midr, side, sido)


def corner_body(par, colse, colso, side, sido):
    even, odd = starts(par, 0, DZ - RZ)
    for start, out in ((even, side), (odd, sido)):

        @pl.loop(0, RZ // 6)
        def _(group):
            for u in range(6):
                k = 6 * group + u
                right, left = pick(par, colse[start + k], colso[start + k])
                out[k] = jnp.concatenate([left, right], axis=0)


def corners(par, colse, colso):
    return pl.pallas_call(
        corner_body,
        out_shape=(PLANES, PLANES),
        in_specs=[SM] + [VM] * 2,
        out_specs=[VM] * 2,
        compiler_params=params(16),
        name="corners",
    )(par, colse, colso)


def weigh_body(planes, blocks, at, labels, kz, kx, yb, out, along_x, inside, views):
    held = labels.shape[1] // 2
    lane = lax.broadcasted_iota(jnp.int32, (1, NY), 1)
    boxes = kx[...]
    for i in range(1, BX):
        boxes = boxes + pltpu.roll(kx[...], i, 1)
    along_x[...] = jnp.zeros(along_x.shape, jnp.float32)
    inside[...] = jnp.zeros(inside.shape, jnp.float32)
    views[...] = jnp.full(views.shape, -1, jnp.int32)

    @pl.loop(0, labels.shape[0])
    def _(holder):
        for k in range(held):
            pair = labels[holder, k]
            shift = labels[holder, held + k]
            view = pair // blocks
            beside = pair % blocks - at[0] * BLK_DEV

            @pl.when((beside >= -2) & (beside < BLK_DEV + 2))
            def _():
                row = holder * held + k
                box = jnp.zeros((1, NY), jnp.float32)
                for v in range(V):
                    box = jnp.where(view == v, boxes[v : v + 1], box)
                step = (BX * beside - 15 + NY) % NY
                moved = pltpu.roll(jnp.broadcast_to(box, (8, NY)), step, 1)
                along_x[pl.ds(row, 1), :] = moved[:1]
                seen = (lane >= shift) & (lane < NY + shift)
                inside[pl.ds(row, 1), :] = jnp.where(seen, 1.0, 0.0)
                views[pl.ds(row, 1), :] = jnp.full((1, NY), view, jnp.int32)

    z = at[1] * DZ + lax.broadcasted_iota(jnp.int32, (DZ, NY), 0)
    tap = lax.broadcasted_iota(jnp.int32, (DZ, NY), 1)
    reached = (z - tap + RZ >= 0) & (z - tap + RZ < planes)
    seen = inside[...].astype(jnp.bfloat16)
    gains, slopes = [], []
    for v in range(V):
        first, second = halves(mul(seen, yb[v, :NY]))
        member = jnp.where(views[...] == v, along_x[...], 0.0)
        gains.append(
            lax.dot_general(
                member.T[:DX],
                first + second,
                (((1,), (0,)), ((), ())),
                precision=exact_mode,
                preferred_element_type=jnp.float32,
            )
        )
        row = jnp.where(reached, jnp.broadcast_to(kz[v : v + 1], (DZ, NY)), 0.0)
        slopes.append(jnp.broadcast_to(jnp.sum(row, axis=1, keepdims=True), (DZ, NY)))
    for i in range(DZ):
        total = slopes[0][i : i + 1] * gains[0]
        for v in range(1, V):
            total = total + slopes[v][i : i + 1] * gains[v]
        out[i] = jnp.maximum(total, 1.0)


def weigh(planes, blocks, at, labels, kz, kx, yb):
    count = labels.shape[0] * labels.shape[1] // 2
    return pl.pallas_call(
        functools.partial(weigh_body, planes, blocks),
        out_shape=f32(DZ, DX, NY),
        in_specs=[SM] * 2 + [VM] * 3,
        out_specs=VM,
        scratch_shapes=[
            pltpu.VMEM((count, NY), jnp.float32),
            pltpu.VMEM((count, NY), jnp.float32),
            pltpu.VMEM((count, NY), jnp.int32),
        ],
        compiler_params=params(16),
        name="weigh",
    )(at, labels, kz, kx, yb)


def gather_total(par, midc, cene, ceno, colse, colso, new):
    even, odd = starts(par, 0, DZ - RZ)

    @pl.loop(0, DZ // 4)
    def _(group):
        for u in range(4):
            z = 4 * group + u
            right, left = pick(par, colse[z], colso[z])
            new[z] = midc[z] + jnp.concatenate([left, right], axis=0)

    for start, centre in ((even, cene), (odd, ceno)):

        @pl.loop(0, RZ // 6)
        def _(group):
            for u in range(6):
                new[start + 6 * group + u] += centre[6 * group + u]


def update_body(par, est, weight, midc, cene, ceno, colse, colso, new, *outs):
    gather_total(par, midc, cene, ceno, colse, colso, new)

    @pl.loop(0, DZ // 4)
    def _(group):
        for u in range(4):
            z = 4 * group + u
            value = est[z] * new[z] / weight[z]
            new[z] = value
            outs[0][z], outs[1][z] = pick(par, value[RX:], value[:RX])

    even, odd = starts(par, 0, DZ - RZ)

    @pl.loop(0, RZ // 6)
    def _(group):
        for u in range(6):
            k = 6 * group + u
            outs[2][k] = new[even + k]
            outs[3][k] = new[odd + k]


def finish_body(par, est, weight, midc, cene, ceno, colse, colso, out, new, sem):
    gather_total(par, midc, cene, ceno, colse, colso, new)
    chunk = 16

    def push(k):
        part = pl.ds(chunk * k, chunk)
        return pltpu.make_async_copy(new.at[part], out.at[part], sem.at[k])

    for k in range(DZ // chunk):

        @pl.loop(0, chunk // 4)
        def _(group):
            for u in range(4):
                z = chunk * k + 4 * group + u
                new[z] = est[z] * new[z] / weight[z]

        push(k).start()
    for k in range(DZ // chunk):
        push(k).wait()


def update(par, est, weight, midc, cene, ceno, colse, colso, last):
    whole = f32(DZ, DX, NY)
    if last:
        call = pl.pallas_call(
            finish_body,
            out_shape=whole,
            in_specs=[SM] + [VM] * 7,
            out_specs=HB,
            scratch_shapes=[
                pltpu.VMEM((DZ, DX, NY), jnp.float32),
                pltpu.SemaphoreType.DMA((DZ // 16,)),
            ],
            compiler_params=params(16),
            name="finish",
        )
    else:
        call = pl.pallas_call(
            update_body,
            out_shape=(whole, COLUMNS, COLUMNS, PLANES, PLANES),
            in_specs=[SM] + [VM] * 7,
            out_specs=[VM] * 5,
            compiler_params=params(16),
            name="update",
        )
    return call(par, est, weight, midc, cene, ceno, colse, colso)


def band(row, rows, first):
    table = jnp.broadcast_to(row, (rows, row.shape[1]))
    return pltpu.roll(table, first % row.shape[1], 1, stride=1, stride_axis=0)


def tables_body(kz, kx, ky, xf, fx, zf, zb, yf, yb):
    for view in range(V):
        full = band(kz[view : view + 1], DZ, PZ - RZ)
        high, low = split(full)
        zf[view] = jnp.concatenate(
            [jnp.concatenate([high, high], axis=1), jnp.concatenate([low, low], axis=1)], axis=0
        )
        high, low = split(full.T)
        zb[view] = jnp.concatenate([high, high, low], axis=1)
        full = band(ky[view : view + 1], NY, -15)[:, :NY]
        high, low = split(full)
        half = jnp.concatenate([high, low], axis=1)
        yb[view] = jnp.concatenate([half, half], axis=0)
        high, low = split(full.T)
        half = jnp.concatenate([high, low], axis=1)
        yf[view] = jnp.concatenate([half, half], axis=0)
    full = jnp.concatenate([band(kx[v : v + 1], DX, RX - 15) for v in range(V)], axis=0)
    fx[...] = full.reshape(V * BLK_DEV, BX, NY)
    high, low = split(full[:, :EX])
    xf[...] = jnp.concatenate([high, high, low], axis=1)


def padded(kernel, lanes):
    return jnp.pad(kernel, ((0, 8 - V), (0, lanes - kernel.shape[1])))


def make_tables(kernel_z, kernel_x, kernel_y):
    def bf16(*shape):
        return jax.ShapeDtypeStruct(shape, jnp.bfloat16)

    return pl.pallas_call(
        tables_body,
        out_shape=(
            bf16(ROWS, 3 * EX),
            f32(V * BLK_DEV, BX, NY),
            bf16(V, 2 * DZ, 2 * EZ),
            bf16(V, EZ, 3 * DZ),
            bf16(V, 2 * NY, 2 * NY),
            bf16(V, 2 * NY, 2 * NY),
        ),
        in_specs=[VM] * 3,
        out_specs=[VM] * 6,
        compiler_params=params(32),
        name="tables",
    )(kernel_z, kernel_x, kernel_y)


def swap(even, odd, axis):
    count = lax.axis_size(axis)
    out = []
    for value, first in ((odd, 1), (even, 0)):
        pairs = []
        for i in range(first, count - 1, 2):
            pairs += [(i, i + 1), (i + 1, i)]
        out.append(lax.ppermute(value, axis, pairs))
    return out[::-1]


def local(estimate0, tiles, psf_z, psf_x, psf_y, tile_pair, tile_shift):
    owners = lax.axis_size("blocks")
    all_blocks = BLK_DEV * owners
    me = lax.axis_index("blocks")
    kernel_z = padded(psf_z / jnp.sum(psf_z, axis=1, keepdims=True), 128)
    kernel_x = padded(psf_x / jnp.sum(psf_x, axis=1, keepdims=True), 128)
    kernel_y = padded(psf_y / jnp.sum(psf_y, axis=1, keepdims=True), 256)

    held = tile_pair % all_blocks // BLK_DEV
    est = estimate0
    par = jnp.stack([me % 2, lax.axis_index("depth") % 2]).astype(jnp.int32)
    columns = swap(*first(columns_body, "first_columns", COLUMNS, par, est), "blocks")
    cene, ceno = first(planes_body, "first_planes", PLANES, par, est)
    sent = place(held, tile_pair, tile_shift, tiles, owners)
    sent, *columns = lax.optimization_barrier((sent, *columns))
    got = lax.all_to_all(sent, "blocks", split_axis=0, concat_axis=0, tiled=True)
    tables = make_tables(kernel_z, kernel_x, kernel_y)

    count = tiles.shape[0]
    labels = got[:, BX * DZ, : 2 * count].astype(jnp.int32)
    pairs, shifts = labels[:, :count], labels[:, count:]
    mine = pairs % all_blocks // BLK_DEV == me
    live = jnp.max(mine.astype(jnp.int32), axis=1)
    got_pair = jnp.sum(jnp.where(mine, pairs, 0), axis=1)
    view = got_pair // all_blocks
    cell = jnp.where(live > 0, view * BLK_DEV + got_pair % all_blocks - me * BLK_DEV, V * BLK_DEV)
    end = lambda value: jnp.full((1,), value, jnp.int32)
    meta = jnp.concatenate([live, end(0), view, end(0), cell, end(V * BLK_DEV)])
    meta = meta.astype(jnp.int32)
    at = jnp.stack([me, lax.axis_index("depth")]).astype(jnp.int32)
    planes = lax.axis_size("depth") * DZ
    weight = weigh(planes, all_blocks, at, labels, kernel_z, kernel_x, tables[5])

    for iteration in range(ITERS):
        centre = swap(cene, ceno, "depth")
        sides = swap(*corners(par, *columns), "depth")
        pieces = (est, *columns, *centre, *sides)
        if iteration == 0:
            spread = spread_ratio(par, meta, blur_all(par, pieces, tables), got, tables)
        else:
            spread = sweep(par, meta, pieces, got, tables)
        midc, midl, midr, cene, ceno, side, sido = spread
        side, sido = swap(side, sido, "depth")
        rims = fold_rims(par, midl, midr, side, sido)
        cene, ceno, *rims = lax.optimization_barrier((cene, ceno, *rims))
        columns = swap(*rims, "blocks")
        cene, ceno = swap(cene, ceno, "depth")
        last = iteration == ITERS - 1
        new = update(par, est, weight, midc, cene, ceno, *columns, last)
        if last:
            return new
        est, *columns, cene, ceno = new
        columns = swap(*columns, "blocks")


def solution(mesh):
    in_specs = (
        P("depth", "blocks", None),
        P("blocks", "depth", None, None),
        P(),
        P(),
        P(),
        P("blocks"),
        P("blocks"),
    )
    out_specs = P("depth", "blocks", None)
    return jax.shard_map(local, mesh=mesh, in_specs=in_specs, out_specs=out_specs, check_vma=False)
```

```python
import functools

import jax
import jax.numpy as jnp
from jax import lax
from jax.experimental import pallas as pl
from jax.experimental.pallas import tpu as pltpu
from jax.sharding import PartitionSpec as P

BLK_DEV = 4
BX = 8
OFF = 8
ITERS = 2
V = 6
NY = 128
DZ = 64
DX = 32
RZ = 30
PZ = 32
RX = 16
EZ = DZ + 2 * PZ
EX = DX + 2 * RX
ROWS = V * DX
MIB = 1 << 20

exact_mode = lax.Precision.HIGHEST


def split(value):
    high = value.astype(jnp.bfloat16)
    low = (value - high.astype(jnp.float32)).astype(jnp.bfloat16)
    return high, low


def mul(a, b):
    return jnp.dot(a, b, preferred_element_type=jnp.float32)


def pair_columns(value, rows):
    return value[:, : value.shape[1] // 2], value[:, value.shape[1] // 2 :]


def blur_x(xf, planes, store):
    both = jnp.concatenate(planes, axis=1)
    high, low = split(both)
    out = mul(xf, jnp.concatenate([high, low, high], axis=0))
    store(out[:, :NY], out[:, NY:])


def starts(par, first, last):
    even = jnp.where(par[1] == 0, last, first)
    return even, first + last - even


def forward_x(par, s_ref, xf_ref, est, colse, colso, cene, ceno, side, sido):
    zeros = jnp.zeros((2,) + s_ref.shape[1:], jnp.float32)
    s_ref[0:2] = zeros
    s_ref[EZ - 2 : EZ] = zeros
    plain = par[0] == 0

    def put(base):
        def store(first, second):
            s_ref[base] = first
            s_ref[base + 1] = second

        return store

    def rim(centre, sides, start):
        @pl.loop(0, RZ // 30)
        def _(group):
            for u in range(15):
                at = 30 * group + 2 * u
                planes = []
                for z in (at, at + 1):
                    planes.append(
                        jnp.concatenate([sides[z, :RX], centre[z], sides[z, RX:]], axis=0)
                    )
                blur_x(xf_ref[...], planes, put(start + at))

    @pl.loop(0, DZ // 64)
    def _(group):
        for u in range(32):
            at = 64 * group + 2 * u
            planes = []
            for z in (at, at + 1):
                even, odd = colse[z], colso[z]
                left, right = jnp.where(plain, odd, even), jnp.where(plain, even, odd)
                planes.append(jnp.concatenate([left, est[z], right], axis=0))
            blur_x(xf_ref[...], planes, put(PZ + at))

    even, odd = starts(par, PZ - RZ, PZ + DZ)
    rim(cene, side, even)
    rim(ceno, sido, odd)


def halves(value):
    middle = value.shape[1] // 2
    return value[:, :middle], value[:, middle:]


def forward_tile(s_ref, zf_ref, yf_ref, view, row):
    field = jnp.swapaxes(s_ref[:, pl.ds(row, BX), :], 0, 1)
    parts = []
    for p in range(BX // 2):
        high, low = split(jnp.concatenate([field[2 * p], field[2 * p + 1]], axis=1))
        out = mul(zf_ref[view], jnp.concatenate([high, low], axis=0))
        parts += halves(out[:DZ] + out[DZ:])
    high, low = split(jnp.concatenate(parts, axis=0))
    first, second = halves(mul(jnp.concatenate([high, low], axis=1), yf_ref[view]))
    return first + second


def backward_tile(zb_ref, yb_ref, view, ratio):
    high, low = split(ratio)
    first, second = halves(mul(jnp.concatenate([high, low], axis=1), yb_ref[view]))
    out = first + second
    parts = []
    for p in range(BX // 2):
        at = 2 * p * DZ
        high, low = split(jnp.concatenate([out[at : at + DZ], out[at + DZ : at + 2 * DZ]], axis=1))
        parts += halves(mul(zb_ref[view], jnp.concatenate([high, low, high], axis=0)))
    return jnp.swapaxes(jnp.stack(parts, axis=0), 0, 1)


def spread_pair(s_ref, xb_ref, base):
    both = jnp.concatenate([s_ref[base], s_ref[base + 1]], axis=1)
    high, low = split(both)
    out = mul(xb_ref[...], jnp.concatenate([high, low], axis=0))
    return halves(out[:EX] + out[EX:])


def backward_rims(par, s_ref, xb_ref, cene, ceno, side, sido):
    def rim(centre, sides, start):
        @pl.loop(0, RZ // 30)
        def _(group):
            for u in range(15):
                at = 30 * group + 2 * u
                for i, plane in enumerate(spread_pair(s_ref, xb_ref, start + at)):
                    sides[at + i] = jnp.concatenate([plane[:RX], plane[RX + DX :]], axis=0)
                    centre[at + i] = plane[RX : RX + DX]

    even, odd = starts(par, PZ - RZ, PZ + DZ)
    rim(cene, side, even)
    rim(ceno, sido, odd)


def middle_body(s_ref, xb_ref, midc, midl, midr):
    @pl.loop(0, DZ // 64)
    def _(group):
        for u in range(32):
            at = 64 * group + 2 * u
            for i, plane in enumerate(spread_pair(s_ref, xb_ref, PZ + at)):
                midl[at + i] = plane[:RX]
                midc[at + i] = plane[RX : RX + DX]
                midr[at + i] = plane[RX + DX :]


def compact(slots, meta, order):
    count = jnp.int32(0)
    for slot in range(slots):
        order[count] = slot
        count = count + meta[slot]
    order[count] = slots
    return count


def gather_x(slots, meta, order, count, fx, picked, xf, xb):
    for n in range(slots):
        slot = jnp.where(n < count, order[n], slots)
        cell = jnp.where(n < count, meta[2 * (slots + 1) + slot], 0)
        scale = jnp.where(n < count, 1.0, 0.0)
        picked[n * BX : (n + 1) * BX] = fx[cell] * scale
    table = picked[...]
    if xf is not None:
        high, low = split(table[:, :EX])
        xf[...] = jnp.concatenate([high, high, low], axis=1)
    high, low = split(table.T[:EX])
    both = jnp.concatenate([high, low], axis=0)
    xb[...] = jnp.concatenate([both, both], axis=1)


def clear_rest(slots, count, s_ref):
    @pl.loop(count, slots)
    def _(n):
        s_ref[:, pl.ds(pl.multiple_of(n * BX, BX), BX), :] = jnp.zeros((EZ, BX, NY), jnp.float32)


def fetches(slots, meta, order, moves):
    count = compact(slots, meta, order)

    @pl.loop(0, count)
    def _(k):
        slot = order[k]
        for make in moves:
            make(slot, meta[2 * (slots + 1) + slot]).start()

    def arrive(slot):
        @pl.when(slot < slots)
        def _():
            for make in moves:
                make(slot, meta[2 * (slots + 1) + slot]).wait()

    return count, arrive


def slots_of(step, k, slots, order, count):
    return [jnp.where(step * k + i < count, order[step * k + i], slots) for i in range(step)]


def blur_tiles(step, slots, meta, order, count, s_ref, zf, yf, held):
    @pl.loop(0, (count + step - 1) // step)
    def _(k):
        slot = slots_of(step, k, slots, order, count)
        out = []
        for i in range(step):
            row = pl.multiple_of((step * k + i) * BX, BX)
            out.append(forward_tile(s_ref, zf, yf, meta[slots + 1 + slot[i]], row))
        for i in range(step):
            held[slot[i]] = out[i]


def visit_tiles(step, slots, meta, order, count, arrive, s_ref, data, zb, yb, predict):
    @pl.loop(0, (count + step - 1) // step)
    def _(k):
        slot = slots_of(step, k, slots, order, count)
        for i in slot:
            arrive(i)
        view = [meta[slots + 1 + i] for i in slot]
        row = [pl.multiple_of((step * k + i) * BX, BX) for i in range(step)]
        blurred = [predict(slot[i], view[i], row[i]) for i in range(step)]
        out = [
            backward_tile(zb, yb, view[i], data[slot[i]] / blurred[i]) for i in range(step)
        ]
        for i in range(step):
            s_ref[:, pl.ds(row[i], BX), :] = out[i]


def data_move(got, data, sem):
    def make(slot, cell):
        return pltpu.make_async_copy(
            got.at[slot, pl.ds(0, BX * DZ)], data.at[slot], sem.at[slot]
        )

    return make


def sweep_body(slots, par, meta, est, colse, colso, cene, ceno, side, sido, got, fx, zf, zb, yf,
               yb, ocene, oceno, oside, osido, s_ref, xb, order, data, sem, picked, xf, held):
    count, arrive = fetches(slots, meta, order, [data_move(got, data, sem)])
    gather_x(slots, meta, order, count, fx, picked, xf, xb)
    forward_x(par, s_ref, xf, est, colse, colso, cene, ceno, side, sido)

    blur_tiles(4, slots, meta, order, count, s_ref, zf, yf, held)

    def predict(slot, view, row):
        return held[slot]

    visit_tiles(4, slots, meta, order, count, arrive, s_ref, data, zb, yb, predict)
    clear_rest(slots, count, s_ref)
    backward_rims(par, s_ref, xb, ocene, oceno, oside, osido)


def blur_body(par, est, colse, colso, cene, ceno, side, sido, xf, zf, yf, out, s_ref, staged, sem):
    forward_x(par, s_ref, xf, est, colse, colso, cene, ceno, side, sido)

    def push(k):
        return pltpu.make_async_copy(
            staged.at[pl.ds(2 * k, 2)], out.at[pl.ds(2 * k, 2)], sem.at[k]
        )

    @pl.loop(0, V)
    def _(view):
        for i in range(BLK_DEV):
            cell = view * BLK_DEV + i
            staged[cell] = forward_tile(s_ref, zf, yf, view, pl.multiple_of(cell * BX, BX))
        push(2 * view).start()
        push(2 * view + 1).start()

    @pl.loop(0, V * BLK_DEV // 2)
    def _(k):
        push(k).wait()


def spread_body(slots, par, meta, blurred, got, far_fx, far_zb, far_yb,
                ocene, oceno, oside, osido, s_ref, xb, order, data, sem, picked, held, held_sem, fx, zb, yb, table_sem):
    tables = [
        pltpu.make_async_copy(far, close, table_sem.at[i])
        for i, (far, close) in enumerate(((far_fx, fx), (far_zb, zb), (far_yb, yb)))
    ]
    for copy in tables:
        copy.start()

    def make(slot, cell):
        return pltpu.make_async_copy(blurred.at[cell], held.at[slot], held_sem.at[slot])

    count, arrive = fetches(slots, meta, order, [make, data_move(got, data, sem)])
    for copy in tables:
        copy.wait()
    gather_x(slots, meta, order, count, fx, picked, None, xb)

    def predict(slot, view, row):
        return held[slot]

    visit_tiles(4, slots, meta, order, count, arrive, s_ref, data, zb, yb, predict)
    clear_rest(slots, count, s_ref)
    backward_rims(par, s_ref, xb, ocene, oceno, oside, osido)


def f32(*shape):
    return jax.ShapeDtypeStruct(shape, jnp.float32)


VM = pl.BlockSpec(memory_space=pltpu.VMEM)
SM = pl.BlockSpec(memory_space=pltpu.SMEM)
PIECES = (
    f32(DZ, DX, NY),
    f32(DZ, RX, NY),
    f32(DZ, RX, NY),
    f32(RZ, DX, NY),
    f32(RZ, DX, NY),
    f32(RZ, 2 * RX, NY),
    f32(RZ, 2 * RX, NY),
)


def params(mib):
    return pltpu.CompilerParams(vmem_limit_bytes=mib * MIB)


def visit_scratch(slots):
    rows = slots * BX
    return [
        pltpu.SMEM((slots + 1,), jnp.int32),
        pltpu.VMEM((slots + 1, BX * DZ, NY), jnp.float32),
        pltpu.SemaphoreType.DMA((slots + 1,)),
        pltpu.VMEM((rows, NY), jnp.float32),
    ]


HB = pl.BlockSpec(memory_space=pltpu.HBM)


def in_hbm(value):
    return pltpu.with_memory_space_constraint(value, pltpu.HBM)


def spread_shapes(slots):
    rows = slots * BX
    return PIECES[3:] + (
        pltpu.VMEM((EZ, rows, NY), jnp.float32),
        pltpu.VMEM((2 * EX, 2 * rows), jnp.bfloat16),
    )


def middle(field, table):
    return pl.pallas_call(
        middle_body,
        out_shape=(PIECES[0], PIECES[1], PIECES[2]),
        in_specs=[VM] * 2,
        out_specs=[VM] * 3,
        compiler_params=params(16),
        name="middle",
    )(field, table)


def sweep(par, meta, pieces, got, tables):
    slots = got.shape[0]
    return pl.pallas_call(
        functools.partial(sweep_body, slots),
        out_shape=spread_shapes(slots),
        in_specs=[SM] * 2 + [VM] * 7 + [HB] + [VM] * 5,
        out_specs=[VM] * 6,
        scratch_shapes=visit_scratch(slots)
        + [
            pltpu.VMEM((slots * BX, 3 * EX), jnp.bfloat16),
            pltpu.VMEM((slots + 1, BX * DZ, NY), jnp.float32),
        ],
        compiler_params=params(28),
        name="sweep",
    )(par, meta, *pieces, in_hbm(got), *tables[1:])


def blur_all(par, pieces, tables):
    xf, fx, zf, zb, yf, yb = tables
    cells = V * BLK_DEV
    return pl.pallas_call(
        blur_body,
        out_shape=pltpu.HBM((cells, BX * DZ, NY), jnp.float32),
        in_specs=[SM] + [VM] * 10,
        out_specs=HB,
        scratch_shapes=[
            pltpu.VMEM((EZ, ROWS, NY), jnp.float32),
            pltpu.VMEM((cells, BX * DZ, NY), jnp.float32),
            pltpu.SemaphoreType.DMA((cells // 2,)),
        ],
        compiler_params=params(34),
        name="blur_all",
    )(par, *pieces, xf, zf, yf)


def spread_ratio(par, meta, blurred, got, tables):
    slots = got.shape[0]
    xf, fx, zf, zb, yf, yb = tables
    return pl.pallas_call(
        functools.partial(spread_body, slots),
        out_shape=spread_shapes(slots),
        in_specs=[SM] * 2 + [HB] * 5,
        out_specs=[VM] * 6,
        scratch_shapes=visit_scratch(slots)
        + [
            pltpu.VMEM((slots + 1, BX * DZ, NY), jnp.float32),
            pltpu.SemaphoreType.DMA((slots + 1,)),
        ]
        + [pltpu.VMEM(table.shape, table.dtype) for table in (fx, zb, yb)]
        + [pltpu.SemaphoreType.DMA((3,))],
        compiler_params=params(28),
        name="spread_ratio",
    )(par, meta, *[in_hbm(value) for value in (blurred, got, fx, zb, yb)])


def place_body(owner, pair, shift, tiles, out, staged, labels, sem, label_sem):
    count = tiles.shape[0]
    slots = out.shape[0]
    lane = lax.broadcasted_iota(jnp.int32, (8, NY), 1)
    values = jnp.zeros((8, NY), jnp.int32)
    for k in range(count):
        values = jnp.where(lane == k, pair[k], values)
        values = jnp.where(lane == count + k, shift[k], values)
    labels[...] = values.astype(jnp.float32)
    copies = []
    for slot in range(slots):
        copies.append(
            pltpu.make_async_copy(
                labels, out.at[slot, pl.ds(BX * DZ, 8)], label_sem.at[slot]
            )
        )
        copies[-1].start()
    column = lax.broadcasted_iota(jnp.int32, (DZ, BX, NY), 2)
    for k in range(count):
        moved = pltpu.roll(tiles[k], (shift[k] + NY) % NY, 2)
        source = column - shift[k]
        moved = jnp.where((source >= 0) & (source < NY), moved, 0.0)
        staged[k] = jnp.swapaxes(moved, 0, 1).reshape(BX * DZ, NY)
        copies.append(
            pltpu.make_async_copy(staged.at[k], out.at[owner[k], pl.ds(0, BX * DZ)], sem.at[k])
        )
        copies[-1].start()
    for copy in copies:
        copy.wait()


def place(owner, pair, shift, tiles, slots):
    count = tiles.shape[0]
    return pl.pallas_call(
        place_body,
        out_shape=pltpu.HBM((slots, BX * DZ + 8, NY), jnp.float32),
        in_specs=[SM, SM, SM, VM],
        out_specs=HB,
        scratch_shapes=[
            pltpu.VMEM((count, BX * DZ, NY), jnp.float32),
            pltpu.VMEM((8, NY), jnp.float32),
            pltpu.SemaphoreType.DMA((count,)),
            pltpu.SemaphoreType.DMA((slots,)),
        ],
        compiler_params=params(32),
        name="place",
    )(owner, pair, shift, tiles)


def pick(par, even_if_plain, other):
    plain = par[0] == 0
    return jnp.where(plain, even_if_plain, other), jnp.where(plain, other, even_if_plain)


def pull(pairs, sem):
    copies = [
        pltpu.make_async_copy(source, target, sem.at[i])
        for i, (source, target) in enumerate(pairs)
    ]
    for copy in copies:
        copy.start()
    for copy in copies:
        copy.wait()


def columns_body(par, est, colse, colso, sem):
    even = pl.multiple_of(jnp.where(par[0] == 0, RX, 0), RX)
    odd = pl.multiple_of(RX - even, RX)
    pull([(est.at[:, pl.ds(even, RX)], colse), (est.at[:, pl.ds(odd, RX)], colso)], sem)


def planes_body(par, est, cene, ceno, sem):
    even, odd = starts(par, 0, DZ - RZ)
    pull([(est.at[pl.ds(even, RZ)], cene), (est.at[pl.ds(odd, RZ)], ceno)], sem)


COLUMNS = f32(DZ, RX, NY)
PLANES = f32(RZ, DX, NY)


def first(body, name, shape, par, est):
    return pl.pallas_call(
        body,
        out_shape=(shape, shape),
        in_specs=[SM, HB],
        out_specs=[VM] * 2,
        scratch_shapes=[pltpu.SemaphoreType.DMA((2,))],
        compiler_params=params(16),
        name=name,
    )(par, in_hbm(est))


def rims_body(par, midl, midr, side, sido, outl, outr):
    even, odd = starts(par, 0, DZ - RZ)

    @pl.loop(0, DZ // 4)
    def _(group):
        for u in range(4):
            z = 4 * group + u
            outl[z], outr[z] = pick(par, midr[z], midl[z])

    for start, sides in ((even, side), (odd, sido)):

        @pl.loop(0, RZ // 6)
        def _(group):
            for u in range(6):
                k = 6 * group + u
                add, other = pick(par, sides[k, RX:], sides[k, :RX])
                outl[start + k] += add
                outr[start + k] += other


def fold_rims(par, midl, midr, side, sido):
    return pl.pallas_call(
        rims_body,
        out_shape=(COLUMNS, COLUMNS),
        in_specs=[SM] + [VM] * 4,
        out_specs=[VM] * 2,
        compiler_params=params(16),
        name="fold_rims",
    )(par, midl, midr, side, sido)


def corner_body(par, colse, colso, side, sido):
    even, odd = starts(par, 0, DZ - RZ)
    for start, out in ((even, side), (odd, sido)):

        @pl.loop(0, RZ // 6)
        def _(group):
            for u in range(6):
                k = 6 * group + u
                right, left = pick(par, colse[start + k], colso[start + k])
                out[k] = jnp.concatenate([left, right], axis=0)


def corners(par, colse, colso):
    return pl.pallas_call(
        corner_body,
        out_shape=(PLANES, PLANES),
        in_specs=[SM] + [VM] * 2,
        out_specs=[VM] * 2,
        compiler_params=params(16),
        name="corners",
    )(par, colse, colso)


def weigh_body(planes, blocks, at, labels, kz, kx, yb, out, along_x, inside, views):
    held = labels.shape[1] // 2
    lane = lax.broadcasted_iota(jnp.int32, (1, NY), 1)
    boxes = kx[...]
    for i in range(1, BX):
        boxes = boxes + pltpu.roll(kx[...], i, 1)
    along_x[...] = jnp.zeros(along_x.shape, jnp.float32)
    inside[...] = jnp.zeros(inside.shape, jnp.float32)
    views[...] = jnp.full(views.shape, -1, jnp.int32)

    @pl.loop(0, labels.shape[0])
    def _(holder):
        for k in range(held):
            pair = labels[holder, k]
            shift = labels[holder, held + k]
            view = pair // blocks
            beside = pair % blocks - at[0] * BLK_DEV

            @pl.when((beside >= -2) & (beside < BLK_DEV + 2))
            def _():
                row = holder * held + k
                box = jnp.zeros((1, NY), jnp.float32)
                for v in range(V):
                    box = jnp.where(view == v, boxes[v : v + 1], box)
                step = (BX * beside - 15 + NY) % NY
                moved = pltpu.roll(jnp.broadcast_to(box, (8, NY)), step, 1)
                along_x[pl.ds(row, 1), :] = moved[:1]
                seen = (lane >= shift) & (lane < NY + shift)
                inside[pl.ds(row, 1), :] = jnp.where(seen, 1.0, 0.0)
                views[pl.ds(row, 1), :] = jnp.full((1, NY), view, jnp.int32)

    z = at[1] * DZ + lax.broadcasted_iota(jnp.int32, (DZ, NY), 0)
    tap = lax.broadcasted_iota(jnp.int32, (DZ, NY), 1)
    reached = (z - tap + RZ >= 0) & (z - tap + RZ < planes)
    seen = inside[...].astype(jnp.bfloat16)
    gains, slopes = [], []
    for v in range(V):
        first, second = halves(mul(seen, yb[v, :NY]))
        member = jnp.where(views[...] == v, along_x[...], 0.0)
        gains.append(
            lax.dot_general(
                member.T[:DX],
                first + second,
                (((1,), (0,)), ((), ())),
                precision=exact_mode,
                preferred_element_type=jnp.float32,
            )
        )
        row = jnp.where(reached, jnp.broadcast_to(kz[v : v + 1], (DZ, NY)), 0.0)
        slopes.append(jnp.broadcast_to(jnp.sum(row, axis=1, keepdims=True), (DZ, NY)))
    for i in range(DZ):
        total = slopes[0][i : i + 1] * gains[0]
        for v in range(1, V):
            total = total + slopes[v][i : i + 1] * gains[v]
        out[i] = jnp.maximum(total, 1.0)


def weigh(planes, blocks, at, labels, kz, kx, yb):
    count = labels.shape[0] * labels.shape[1] // 2
    return pl.pallas_call(
        functools.partial(weigh_body, planes, blocks),
        out_shape=f32(DZ, DX, NY),
        in_specs=[SM] * 2 + [VM] * 3,
        out_specs=VM,
        scratch_shapes=[
            pltpu.VMEM((count, NY), jnp.float32),
            pltpu.VMEM((count, NY), jnp.float32),
            pltpu.VMEM((count, NY), jnp.int32),
        ],
        compiler_params=params(16),
        name="weigh",
    )(at, labels, kz, kx, yb)


def gather_total(par, midc, cene, ceno, colse, colso, new):
    even, odd = starts(par, 0, DZ - RZ)

    @pl.loop(0, DZ // 4)
    def _(group):
        for u in range(4):
            z = 4 * group + u
            right, left = pick(par, colse[z], colso[z])
            new[z] = midc[z] + jnp.concatenate([left, right], axis=0)

    for start, centre in ((even, cene), (odd, ceno)):

        @pl.loop(0, RZ // 6)
        def _(group):
            for u in range(6):
                new[start + 6 * group + u] += centre[6 * group + u]


def update_body(par, est, weight, midc, cene, ceno, colse, colso, new, *outs):
    gather_total(par, midc, cene, ceno, colse, colso, new)

    @pl.loop(0, DZ // 4)
    def _(group):
        for u in range(4):
            z = 4 * group + u
            value = est[z] * new[z] / weight[z]
            new[z] = value
            outs[0][z], outs[1][z] = pick(par, value[RX:], value[:RX])

    even, odd = starts(par, 0, DZ - RZ)

    @pl.loop(0, RZ // 6)
    def _(group):
        for u in range(6):
            k = 6 * group + u
            outs[2][k] = new[even + k]
            outs[3][k] = new[odd + k]


def finish_body(par, est, weight, midc, cene, ceno, colse, colso, out, new, sem):
    gather_total(par, midc, cene, ceno, colse, colso, new)
    chunk = 16

    def push(k):
        part = pl.ds(chunk * k, chunk)
        return pltpu.make_async_copy(new.at[part], out.at[part], sem.at[k])

    for k in range(DZ // chunk):

        @pl.loop(0, chunk // 4)
        def _(group):
            for u in range(4):
                z = chunk * k + 4 * group + u
                new[z] = est[z] * new[z] / weight[z]

        push(k).start()
    for k in range(DZ // chunk):
        push(k).wait()


def update(par, est, weight, midc, cene, ceno, colse, colso, last):
    whole = f32(DZ, DX, NY)
    if last:
        call = pl.pallas_call(
            finish_body,
            out_shape=whole,
            in_specs=[SM] + [VM] * 7,
            out_specs=HB,
            scratch_shapes=[
                pltpu.VMEM((DZ, DX, NY), jnp.float32),
                pltpu.SemaphoreType.DMA((DZ // 16,)),
            ],
            compiler_params=params(16),
            name="finish",
        )
    else:
        call = pl.pallas_call(
            update_body,
            out_shape=(whole, COLUMNS, COLUMNS, PLANES, PLANES),
            in_specs=[SM] + [VM] * 7,
            out_specs=[VM] * 5,
            compiler_params=params(16),
            name="update",
        )
    return call(par, est, weight, midc, cene, ceno, colse, colso)


def band(row, rows, first):
    table = jnp.broadcast_to(row, (rows, row.shape[1]))
    return pltpu.roll(table, first % row.shape[1], 1, stride=1, stride_axis=0)


def tables_body(kz, kx, ky, xf, fx, zf, zb, yf, yb):
    for view in range(V):
        full = band(kz[view : view + 1], DZ, PZ - RZ)
        high, low = split(full)
        zf[view] = jnp.concatenate(
            [jnp.concatenate([high, high], axis=1), jnp.concatenate([low, low], axis=1)], axis=0
        )
        high, low = split(full.T)
        zb[view] = jnp.concatenate([high, high, low], axis=1)
        full = band(ky[view : view + 1], NY, -15)[:, :NY]
        high, low = split(full)
        half = jnp.concatenate([high, low], axis=1)
        yb[view] = jnp.concatenate([half, half], axis=0)
        high, low = split(full.T)
        half = jnp.concatenate([high, low], axis=1)
        yf[view] = jnp.concatenate([half, half], axis=0)
    full = jnp.concatenate([band(kx[v : v + 1], DX, RX - 15) for v in range(V)], axis=0)
    fx[...] = full.reshape(V * BLK_DEV, BX, NY)
    high, low = split(full[:, :EX])
    xf[...] = jnp.concatenate([high, high, low], axis=1)


def padded(kernel, lanes):
    return jnp.pad(kernel, ((0, 8 - V), (0, lanes - kernel.shape[1])))


def make_tables(kernel_z, kernel_x, kernel_y):
    def bf16(*shape):
        return jax.ShapeDtypeStruct(shape, jnp.bfloat16)

    return pl.pallas_call(
        tables_body,
        out_shape=(
            bf16(ROWS, 3 * EX),
            f32(V * BLK_DEV, BX, NY),
            bf16(V, 2 * DZ, 2 * EZ),
            bf16(V, EZ, 3 * DZ),
            bf16(V, 2 * NY, 2 * NY),
            bf16(V, 2 * NY, 2 * NY),
        ),
        in_specs=[VM] * 3,
        out_specs=[VM] * 6,
        compiler_params=params(32),
        name="tables",
    )(kernel_z, kernel_x, kernel_y)


def swap(even, odd, axis):
    count = lax.axis_size(axis)
    out = []
    for value, first in ((odd, 1), (even, 0)):
        pairs = []
        for i in range(first, count - 1, 2):
            pairs += [(i, i + 1), (i + 1, i)]
        out.append(lax.ppermute(value, axis, pairs))
    return out[::-1]


def local(estimate0, tiles, psf_z, psf_x, psf_y, tile_pair, tile_shift):
    owners = lax.axis_size("blocks")
    all_blocks = BLK_DEV * owners
    me = lax.axis_index("blocks")
    kernel_z = padded(psf_z / jnp.sum(psf_z, axis=1, keepdims=True), 128)
    kernel_x = padded(psf_x / jnp.sum(psf_x, axis=1, keepdims=True), 128)
    kernel_y = padded(psf_y / jnp.sum(psf_y, axis=1, keepdims=True), 256)

    held = tile_pair % all_blocks // BLK_DEV
    est = estimate0
    par = jnp.stack([me % 2, lax.axis_index("depth") % 2]).astype(jnp.int32)
    columns = swap(*first(columns_body, "first_columns", COLUMNS, par, est), "blocks")
    cene, ceno = first(planes_body, "first_planes", PLANES, par, est)
    sent = place(held, tile_pair, tile_shift, tiles, owners)
    sent, *columns = lax.optimization_barrier((sent, *columns))
    got = lax.all_to_all(sent, "blocks", split_axis=0, concat_axis=0, tiled=True)
    tables = make_tables(kernel_z, kernel_x, kernel_y)

    count = tiles.shape[0]
    labels = got[:, BX * DZ, : 2 * count].astype(jnp.int32)
    pairs, shifts = labels[:, :count], labels[:, count:]
    mine = pairs % all_blocks // BLK_DEV == me
    live = jnp.max(mine.astype(jnp.int32), axis=1)
    got_pair = jnp.sum(jnp.where(mine, pairs, 0), axis=1)
    view = got_pair // all_blocks
    cell = jnp.where(live > 0, view * BLK_DEV + got_pair % all_blocks - me * BLK_DEV, V * BLK_DEV)
    end = lambda value: jnp.full((1,), value, jnp.int32)
    meta = jnp.concatenate([live, end(0), view, end(0), cell, end(V * BLK_DEV)])
    meta = meta.astype(jnp.int32)
    at = jnp.stack([me, lax.axis_index("depth")]).astype(jnp.int32)
    planes = lax.axis_size("depth") * DZ
    weight = weigh(planes, all_blocks, at, labels, kernel_z, kernel_x, tables[5])

    for iteration in range(ITERS):
        centre = swap(cene, ceno, "depth")
        sides = swap(*corners(par, *columns), "depth")
        pieces = (est, *columns, *centre, *sides)
        if iteration == 0:
            spread = spread_ratio(par, meta, blur_all(par, pieces, tables), got, tables)
        else:
            spread = sweep(par, meta, pieces, got, tables)
        cene, ceno, side, sido, field, table = spread
        side, sido = swap(side, sido, "depth")
        midc, midl, midr = middle(field, table)
        rims = fold_rims(par, midl, midr, side, sido)
        cene, ceno, *rims = lax.optimization_barrier((cene, ceno, *rims))
        columns = swap(*rims, "blocks")
        cene, ceno = swap(cene, ceno, "depth")
        last = iteration == ITERS - 1
        new = update(par, est, weight, midc, cene, ceno, *columns, last)
        if last:
            return new
        est, *columns, cene, ceno = new
        columns = swap(*columns, "blocks")


def solution(mesh):
    in_specs = (
        P("depth", "blocks", None),
        P("blocks", "depth", None, None),
        P(),
        P(),
        P(),
        P("blocks"),
        P("blocks"),
    )
    out_specs = P("depth", "blocks", None)
    return jax.shard_map(local, mesh=mesh, in_specs=in_specs, out_specs=out_specs, check_vma=False)
```
